256 devices in a mesh: space: 64 (over x, z, core), rep: 4 (over y).
Axes of the slice: x: 4, y: 4, z: 8, core: 2. Of those that a mesh axis runs over, the one named last changes fastest.
Arguments:
- feats: bfloat16 [4, 256, 512, 128], P('rep', 'space'), may hold values from -6 to 6
- w_conv: bfloat16 [27, 128, 128], replicated, may hold values from -0.109375 to 0.109375
- w_down: bfloat16 [8, 128, 128], replicated, may hold values from -0.1875 to 0.1875
- cotangent: bfloat16 [4, 256, 64, 128], P('rep', 'space'), may hold values from -6 to 6
- nbr_owner: int32 [4, 256, 6], P('rep', 'space'), may hold values from -1 to 63, as said below
- nbr_slot: int32 [4, 256, 6], P('rep', 'space'), may hold values from -1 to 3, as said below
Outputs:
- pooled: bfloat16 [4, 256, 64, 128], P('rep', 'space')
- d_feats: bfloat16 [4, 256, 512, 128], P('rep', 'space')
- d_wconv: float32 [27, 128, 128], replicated
- d_wdown: float32 [8, 128, 128], replicated
The draws below stay inside these ranges and needn't reach their ends.
Inputs may be any that keep to these rules, and one draw needn't show every extreme that they name: `nbr_owner`: kernel maps are mutually consistent: if block b has neighbour c in direction +a then c has neighbour b in direction -a, and each block is named at most once a direction. A neighbour's owner lies within 2 space indices of the block's own. In each direction, for each other space index within 2 that exists, exactly 1 of a device's blocks has its neighbour there. `nbr_slot`: slots of listed neighbours; -1 exactly where nbr_owner is -1.
All inputs are finite; a program needn't handle non-finite values.
Results may differ from the reference program's by a relative error of at most 0.0049.
Values may be sent and summed in bfloat16 or wider, within the bound.
A program may use at most 64 MiB of HBM per device.

```python
import jax
import jax.numpy as jnp
from jax import lax

C = 128
NB = 4
CAP = 1
SCENES = 4
BLOCKS = 256
N_SPACE = 64


def neighbour_tables(key):
    pattern = jnp.array([-2, -1, 1, 2], jnp.int32)
    indices = jnp.arange(NB, dtype=jnp.int32)
    devices = jnp.arange(N_SPACE, dtype=jnp.int32)
    owners_all = []
    slots_all = []
    for scene_id in range(SCENES):
        owners_scene = []
        slots_scene = []
        for axis_id in range(3):
            sub_key = jax.random.fold_in(jax.random.fold_in(key, scene_id + 11), axis_id + 5)
            key_order, key_shuffle, key_kept = jax.random.split(sub_key, 3)
            pattern_slot = jnp.where(indices < 4 * CAP, pattern[jnp.minimum(indices // CAP, 3)], 0)
            shifts = pattern_slot[jax.random.permutation(key_order, NB)]
            shuffle = jax.vmap(lambda one_key: jax.random.permutation(one_key, NB))(jax.random.split(key_shuffle, N_SPACE)).astype(jnp.int32)
            kept = (jax.random.randint(key_kept, (N_SPACE, NB), 0, 4) > 0) | (shifts[None, :] != 0)
            targets = devices[:, None] + shifts[None, :]
            present_up = (targets >= 0) & (targets < N_SPACE) & kept
            clipped = jnp.clip(targets, 0, N_SPACE - 1)
            slot_up = shuffle[clipped, jnp.broadcast_to(indices[None, :], (N_SPACE, NB))]
            inverse = jnp.argsort(shuffle, axis=1).astype(jnp.int32)
            source_dev = devices[:, None] - shifts[inverse]
            clipped_src = jnp.clip(source_dev, 0, N_SPACE - 1)
            present_down = (source_dev >= 0) & (source_dev < N_SPACE) & kept[clipped_src, inverse]
            owners_scene.append(jnp.where(present_up, targets, -1))
            owners_scene.append(jnp.where(present_down, source_dev, -1))
            slots_scene.append(jnp.where(present_up, slot_up, -1))
            slots_scene.append(jnp.where(present_down, inverse, -1))
        owners_all.append(jnp.stack(owners_scene, axis=-1).reshape(BLOCKS, 6))
        slots_all.append(jnp.stack(slots_scene, axis=-1).reshape(BLOCKS, 6))
    return (jnp.stack(owners_all).astype(jnp.int32), jnp.stack(slots_all).astype(jnp.int32))


def draw_nbr_owner(key, part):
    return neighbour_tables(key)[0]


def draw_nbr_slot(key, part):
    return neighbour_tables(key)[1]


def level_of(own_key, shape, cuts, smallest, largest):
    factor_of, own = 1.0, jax.random.fold_in(own_key, 6)
    for axis_at, blocks in cuts:
        draws = jnp.exp(jax.random.uniform(jax.random.fold_in(own, axis_at), (blocks,), jnp.float32, smallest / len(cuts), largest / len(cuts)))
        factor_of = factor_of * jnp.repeat(draws, shape[axis_at] // blocks).reshape([-1 if axis == axis_at else 1 for axis in range(len(shape))])
    return factor_of


def gaussian(key, shape, deviation, limit, pieces=(), held_as=jnp.bfloat16):
    gain = level_of(key, shape, pieces, -0.22, 0.18) if pieces else 1.0
    result = jax.random.normal(key, shape, jnp.float32) * deviation * gain
    return jnp.minimum(jnp.maximum(result, -limit), limit).astype(held_as)


def setup_inputs(seed: int = 0) -> dict:
    seeds = jax.random.split(jax.random.key(seed), 7)
    feats = gaussian(seeds[0], (SCENES, BLOCKS, 512, C), 1.0, 6.0, ((0, 4), (1, 64)))
    w_conv = gaussian(seeds[1], (27, C, C), (27 * C) ** -0.5, 0.109375)
    w_down = gaussian(seeds[2], (8, C, C), (8 * C) ** -0.5, 0.1875)
    cotangent = gaussian(seeds[3], (SCENES, BLOCKS, 64, C), 1.0, 6.0, ((0, 4), (1, 64)))
    nbr_owner = draw_nbr_owner(jax.random.fold_in(seeds[6], 71), 0)
    nbr_slot = draw_nbr_slot(jax.random.fold_in(seeds[6], 71), 0)
    return dict(feats=feats, w_conv=w_conv, w_down=w_down, cotangent=cotangent, nbr_owner=nbr_owner, nbr_slot=nbr_slot)


def fetch_faces(face_set, owners, slot_list):
    present = owners >= 0
    indices = jnp.where(present, owners * NB + slot_list, 0).astype(jnp.int32)
    picked = jnp.take(face_set, indices, axis=0)
    return jnp.where(present.reshape(-1, 1, 1, 1), picked, jnp.zeros((), face_set.dtype))

def extend(blocks, owners, slot_list):
    padded = blocks
    for axis_id in range(3):
        along = axis_id + 1
        extent = padded.shape[along]
        plus_face = lax.index_in_dim(padded, extent - 1, along, keepdims=False)
        minus_face = lax.index_in_dim(padded, 0, along, keepdims=False)
        minus_halo = fetch_faces(plus_face, owners[:, 2 * axis_id + 1], slot_list[:, 2 * axis_id + 1])
        plus_halo = fetch_faces(minus_face, owners[:, 2 * axis_id], slot_list[:, 2 * axis_id])
        padded = jnp.concatenate([jnp.expand_dims(minus_halo, along), padded, jnp.expand_dims(plus_halo, along)], axis=along)
    return padded

def convolve(padded, weights):
    width = padded.shape[-1]
    summed = jnp.zeros((padded.shape[0] * 512, width), jnp.float32)
    for tap_id in range(27):
        start_x, start_y, start_z = (tap_id // 9, tap_id // 3 % 3, tap_id % 3)
        window = padded[:, start_x:start_x + 8, start_y:start_y + 8, start_z:start_z + 8, :].reshape(-1, width)
        summed = summed + jnp.dot(window, weights[tap_id], preferred_element_type=jnp.float32)
    return summed

def one_scene(inputs, w_conv, w_down):
    feat_scene, grad_scene, owners, slot_list = inputs
    blocks = feat_scene.reshape(BLOCKS, 8, 8, 8, C)
    padded = extend(blocks, owners, slot_list)
    pre_act = convolve(padded, w_conv)
    hidden = jax.nn.silu(pre_act).astype(jnp.bfloat16)
    hidden_sub = hidden.reshape(BLOCKS, 4, 2, 4, 2, 4, 2, C).astype(jnp.float32)
    down_five = w_down.reshape(2, 2, 2, C, C).astype(jnp.float32)
    pooled = jnp.einsum('bxiyjzkc,ijkcd->bxyzd', hidden_sub, down_five).reshape(BLOCKS, 64, C).astype(jnp.bfloat16)
    grad_out = grad_scene.reshape(BLOCKS, 4, 4, 4, C).astype(jnp.float32)
    grad_down = jnp.einsum('bxiyjzkc,bxyzd->ijkcd', hidden_sub, grad_out).reshape(8, C, C)
    grad_hidden = jnp.einsum('bxyzd,ijkcd->bxiyjzkc', grad_out, down_five).reshape(-1, C)
    sigmoid = jax.nn.sigmoid(pre_act)
    grad_pre = (grad_hidden * sigmoid * (1.0 + pre_act * (1.0 - sigmoid))).astype(jnp.bfloat16)
    grad_pre_f = grad_pre.astype(jnp.float32)
    grad_padded = jnp.zeros((BLOCKS, 10, 10, 10, C), jnp.float32)
    grad_list = []
    for tap_id in range(27):
        start_x, start_y, start_z = (tap_id // 9, tap_id // 3 % 3, tap_id % 3)
        window = padded[:, start_x:start_x + 8, start_y:start_y + 8, start_z:start_z + 8, :].reshape(-1, C)
        grad_list.append(jnp.einsum('rc,rd->cd', window.astype(jnp.float32), grad_pre_f))
        contrib = jnp.dot(grad_pre, w_conv[tap_id].T, preferred_element_type=jnp.float32).reshape(BLOCKS, 8, 8, 8, C)
        grad_padded = grad_padded.at[:, start_x:start_x + 8, start_y:start_y + 8, start_z:start_z + 8, :].add(contrib)
    grad_conv = jnp.stack(grad_list)
    _, pullback = jax.vjp(lambda source: extend(source, owners, slot_list), blocks.astype(jnp.float32))
    d_blocks = pullback(grad_padded)[0]
    d_feats = d_blocks.reshape(BLOCKS, 512, C).astype(jnp.bfloat16)
    return (pooled, d_feats, grad_conv, grad_down)

def reference(feats, w_conv, w_down, cotangent, nbr_owner, nbr_slot):
    pooled, d_feats, grad_conv, grad_down = lax.map(lambda inputs: one_scene(inputs, w_conv, w_down), (feats, cotangent, nbr_owner, nbr_slot))
    norm_factor = 1.0 / jnp.sqrt(jnp.float32(SCENES * BLOCKS * 512))
    d_wconv = lax.optimization_barrier(jnp.sum(grad_conv, axis=0)) * norm_factor
    d_wdown = lax.optimization_barrier(jnp.sum(grad_down, axis=0)) * norm_factor
    return (pooled, d_feats, d_wconv, d_wdown)
```

```python
import jax
import jax.numpy as jnp
import numpy as np
from jax import lax
from jax.experimental import pallas as pl
from jax.experimental.pallas import tpu as pltpu
from jax.sharding import PartitionSpec as P

BF = jnp.bfloat16
F32 = jnp.float32
MESH = pl.DeviceIdType.MESH
SHIFTS = (-2, -1, 1, 2)
N_SPACE = 64
N_PLANE = 16
N_Z = 8


def onehot_tables():
    tables = {}

    def table(name, rows, cols):
        tables[name] = np.zeros((rows, cols), np.float32)
        return tables[name]

    swap = table("swap", 256, 256)
    for p in range(16):
        for q in range(16):
            swap[p * 16 + q, q * 16 + p] = 1
    send_y, recv_y = table("send_y", 192, 256), table("recv_y", 256, 256)
    send_z, recv_z = table("send_z", 256, 384), table("recv_z", 320, 256)
    send_gz, recv_gz = table("send_gz", 128, 128), table("recv_gz", 128, 128)
    send_gy, recv_gy = table("send_gy", 192, 256), table("recv_gy", 160, 256)
    send_gx = table("send_gx", 128, 256)
    low, high = table("low", 256, 256), table("high", 256, 256)
    insert = table("insert", 512, 128)
    for b in range(4):
        for xq in range(4):
            row = xq * 4 + b
            for z in range(8):
                send_y[b * 48 + xq * 8 + z, z * 16 + row] = 1
                recv_y[z * 16 + row, b * 64 + xq * 8 + z] = 1
                far = (xq + 1) * 8 + z if xq < 3 else 40 + z
                recv_y[128 + z * 16 + row, b * 64 + far] = 1
                if xq == 3:
                    send_y[b * 48 + 40 + z, 128 + z * 16 + row] = 1
                send_gz[b * 32 + z * 4 + xq, z * 16 + row] = 1
                recv_gz[z * 16 + row, b * 32 + z * 4 + xq] = 1
            for y in range(10):
                send_z[b * 64 + xq * 10 + y, y * 16 + row] = 1
                recv_z[y * 16 + row, b * 64 + xq * 10 + y] = 1
                far = (xq + 1) * 10 + y if xq < 3 else 40 + y
                recv_z[160 + y * 16 + row, b * 64 + far] = 1
                if xq == 3:
                    send_z[b * 64 + 40 + y, 160 + y * 16 + row] = 1
                send_gy[b * 48 + y * 4 + xq, y * 16 + row] = 1
                recv_gy[y * 16 + row, b * 64 + y * 4 + xq] = 1
            for k in range(16):
                if xq >= 1:
                    low[k * 16 + row, k * 16 + row - 4] = 1
                if xq <= 2:
                    high[k * 16 + row, k * 16 + row + 4] = 1
        for k in range(16):
            send_gx[b * 16 + k, k * 16 + 12 + b] = 1
            send_gx[64 + b * 16 + k, k * 16 + b] = 1
            insert[k * 16 + b, b * 16 + k] = 1
            insert[256 + k * 16 + 12 + b, 64 + b * 16 + k] = 1
    places, parts, start = {}, [], 0
    for name, value in tables.items():
        rows, cols = value.shape
        places[name] = (start, rows, cols)
        parts.append(np.pad(value, ((0, 0), (0, 384 - cols))))
        start += rows
    return places, np.concatenate(parts)


PLACES, TABLES = onehot_tables()


def mm(left, right):
    return jnp.dot(left, right, preferred_element_type=F32)


def mm_nt(left, right):
    return lax.dot_general(left, right, (((1,), (1,)), ((), ())), preferred_element_type=F32)


def kernel(
    feats_h, wc_h, wd_h, cot_h, tab_h, own_s, slot_s,
    pooled_o, dfeats_o, sums_o,
    feats, wc, wd, cot, tab, bf, bg, wf, wb, gh, hid, gpt, cotp, dwf,
    sx, rx, oy, sy, ry, oz, sz, rz, ogz, sgz, rgz, ogy, sgy, rgy, ogx, sgx, rgx,
    s1, r1, s2, r2, r3, fin,
    lsem, hs, hr, cs, cr, xs, xr, zs, zr, as_, ar, fs, fr,
):
    pos = lax.axis_index("space")
    rep = lax.axis_index("rep")
    core = lax.rem(pos, 2)
    zpos = lax.rem(lax.div(pos, 2), 8)
    xpos = lax.div(pos, 16)
    plane = xpos * 4 + rep
    sibling = pos + 1 - 2 * core

    def in_space(to):
        return {"space": to, "rep": rep}

    def in_plane(k):
        to = lax.rem(plane + k, N_PLANE)
        return {"space": lax.div(to, 4) * 16 + lax.rem(pos, 16), "rep": lax.rem(to, 4)}

    def in_z(k):
        to = lax.rem(zpos + k, N_Z)
        return {"space": xpos * 16 + to * 2 + core, "rep": rep}

    loads = [
        pltpu.make_async_copy(src, dst, lsem.at[i])
        for i, (src, dst) in enumerate(
            ((feats_h, feats), (tab_h, tab), (cot_h, cot), (wc_h, wc), (wd_h, wd))
        )
    ]
    for one in loads:
        one.start()

    barrier = pltpu.get_barrier_semaphore()
    for t in SHIFTS:
        to = lax.rem(pos + t + N_SPACE, N_SPACE)
        pl.semaphore_signal(barrier, inc=1, device_id=in_space(to), device_id_type=MESH)
    pl.semaphore_signal(barrier, inc=1, device_id=in_space(sibling), device_id_type=MESH)

    def greet_plane(k, carry):
        pl.semaphore_signal(barrier, inc=1, device_id=in_plane(k), device_id_type=MESH)
        return carry

    def greet_z(k, carry):
        pl.semaphore_signal(barrier, inc=1, device_id=in_z(k), device_id_type=MESH)
        return carry

    lax.fori_loop(1, N_PLANE, greet_plane, 0)
    lax.fori_loop(1, N_Z, greet_z, 0)

    owners = [[own_s[0, b, d] for d in range(6)] for b in range(4)]
    slots = [[slot_s[0, b, d] for d in range(6)] for b in range(4)]

    def pick(d, t):
        found = jnp.int32(0)
        for b in range(1, 4):
            hit = (owners[b][d] == pos + t) & (owners[b][d] >= 0)
            found = jnp.where(hit, b, found)
        return found

    def place(d, b):
        gap = pos - owners[b][d]
        far = jnp.clip(jnp.where(gap < 0, gap + 2, gap + 1), 0, 3)
        near = jnp.clip(5 + slots[b][d], 5, 8)
        return jnp.where(owners[b][d] < 0, 4, jnp.where(gap == 0, near, far))

    for ref in (rx, ry, rz, rgz, rgy, rgx):
        for side in range(2):
            ref[side, 4] = jnp.zeros(ref.shape[2:], BF)

    def halo_copy(phase, side, i, send, recv):
        to = lax.rem(pos + SHIFTS[i] + N_SPACE, N_SPACE)
        return pltpu.make_async_remote_copy(
            src_ref=send.at[side, i],
            dst_ref=recv.at[side, i],
            send_sem=hs.at[phase, side, i],
            recv_sem=hr.at[phase, side, i],
            device_id=in_space(to),
            device_id_type=MESH,
        )

    sent = []

    def halo_send(phase, axis, own, send, recv):
        copies = []
        for side in range(2):
            for i, t in enumerate(SHIFTS):
                send[side, i] = own(side, pick(2 * axis + side, t))
                one = halo_copy(phase, side, i, send, recv)
                one.start()
                copies.append(one)
        sent.extend(copies)
        return copies

    def halo_recv(axis, copies, recv):
        for one in copies:
            one.wait_recv()
        return [
            [recv[side, place(2 * axis + 1 - side, b)] for b in range(4)] for side in range(2)
        ]

    def onehot(name):
        start, rows, cols = PLACES[name]
        return tab[start : start + rows, 0:cols]

    def permuted(name, value):
        return mm(onehot(name), value).astype(BF)

    loads[0].wait()
    for b in range(4):
        rx[0, 5 + b] = feats[b, 448:512, :]
        rx[1, 5 + b] = feats[b, 0:64, :]
    for side in range(2):
        for i, t in enumerate(SHIFTS):
            rows = slice(448, 512) if side == 0 else slice(0, 64)
            sx[side, i] = feats[pick(side, t), rows, :]
    pl.semaphore_wait(barrier, 4 + 1 + N_PLANE - 1 + N_Z - 1)
    copies = [halo_copy(0, side, i, sx, rx) for side in range(2) for i in range(4)]
    for one in copies:
        one.start()
    sent.extend(copies)

    loads[1].wait()

    def x_layer(s, chunk, halo):
        rows = []
        for xq in range(4):
            x = 2 * xq + s - 1
            for b in range(4):
                if x < 0 or x > 7:
                    rows.append(halo[0 if x < 0 else 1][b][16 * chunk : 16 * chunk + 16])
                else:
                    rows.append(feats[b, 64 * x + 16 * chunk : 64 * x + 16 * chunk + 16, :])
        return jnp.concatenate(rows, axis=0)

    def put_rows(ref, y, z, count, lanes, value):
        ref[pl.ds(y * 10 + z, count), :, lanes] = value

    for chunk in range(4):
        both = jnp.concatenate([x_layer(1, chunk, None), x_layer(2, chunk, None)], axis=1)
        out = permuted("swap", both).reshape(2, 8, 16, 256)
        for j in range(2):
            put_rows(bf, 2 * chunk + j + 1, 1, 8, slice(128, 384), out[j])

    halo = halo_recv(0, copies, rx)
    for chunk in range(4):
        both = jnp.concatenate([x_layer(0, chunk, halo), x_layer(3, chunk, halo)], axis=1)
        out = permuted("swap", both).reshape(2, 8, 16, 256)
        for j in range(2):
            put_rows(bf, 2 * chunk + j + 1, 1, 8, slice(0, 128), out[j, :, :, 0:128])
            put_rows(bf, 2 * chunk + j + 1, 1, 8, slice(384, 512), out[j, :, :, 128:256])

    for side in range(2):
        y = 8 if side == 0 else 1
        layer = bf[y * 10 + 1 : y * 10 + 9].reshape(128, 512)
        flat = jnp.concatenate([layer[:, 0:256], layer[:, 256:512]], axis=0)
        faces = permuted("send_y", flat).reshape(4, 48, 256)
        oy[side] = faces
        ry[side, 5:9] = faces
    copies = halo_send(1, 1, lambda side, b: oy[side, b], sy, ry)

    loads[2].wait()
    loads[3].wait()
    loads[4].wait()
    cot_rows = jnp.concatenate(
        [cot[b, 16 * xq : 16 * xq + 16, :] for xq in range(4) for b in range(4)], axis=0
    )
    cot_perm = permuted("swap", cot_rows)
    cotp[...] = cot_perm

    def down_weight(j, k):
        return jnp.concatenate([wd[2 * j + k], wd[4 + 2 * j + k]], axis=0)

    for j in range(2):
        for k in range(2):
            gh[j, k] = mm_nt(cot_perm, down_weight(j, k)).reshape(4, 64, 256)

    def weights(k9, carry):
        for s in range(4):
            for xl in range(2):
                dx = s - xl
                fwd_at = (pl.ds(s * 128, 128), pl.ds(xl * 128, 128))
                bwd_at = (pl.ds(xl * 128, 128), pl.ds(s * 128, 128))
                if 0 <= dx <= 2:
                    wf[(k9,) + fwd_at] = wc[9 * dx + k9]
                    wb[(k9,) + bwd_at] = wc[9 * (2 - dx) + 8 - k9]
                else:
                    wf[(k9,) + fwd_at] = jnp.zeros((128, 128), BF)
                    wb[(k9,) + bwd_at] = jnp.zeros((128, 128), BF)
        return carry

    lax.fori_loop(0, 9, weights, 0)

    def tall(values, rows):
        pad = jnp.zeros((rows - values[0].shape[0], values[0].shape[1]), BF)
        return jnp.concatenate([v for value in values for v in (value, pad)], axis=0)

    halo = halo_recv(1, copies, ry)
    for side in range(2):
        y = 0 if side == 0 else 9
        out = permuted("recv_y", tall(halo[side], 64))
        put_rows(bf, y, 1, 8, slice(0, 256), out[0:128].reshape(8, 16, 256))
        put_rows(bf, y, 1, 8, slice(256, 512), out[128:256].reshape(8, 16, 256))

    for side in range(2):
        z = 8 if side == 0 else 1
        near = [bf[y * 10 + z, :, 0:256] for y in range(10)]
        far = [bf[y * 10 + z, :, 256:512] for y in range(10)]
        flat = jnp.concatenate(near + far + [jnp.zeros((64, 256), BF)], axis=0)
        faces = permuted("send_z", flat).reshape(4, 64, 256)
        oz[side] = faces
        rz[side, 5:9] = faces
    copies = halo_send(2, 2, lambda side, b: oz[side, b], sz, rz)
    bg[100:112] = jnp.zeros((12, 16, 512), BF)
    dwf[2, 1, 5] = jnp.zeros((128, 128), F32)
    halo = halo_recv(2, copies, rz)
    for side in range(2):
        z = 0 if side == 0 else 9
        out = permuted("recv_z", jnp.concatenate(halo[side], axis=0))
        for y in range(10):
            bf[y * 10 + z, :, 0:256] = out[16 * y : 16 * y + 16]
            bf[y * 10 + z, :, 256:512] = out[160 + 16 * y : 160 + 16 * y + 16]

    def window(ref, y, dz):
        lower = ref[pl.ds(y * 10 + dz, 8)]
        upper = ref[pl.ds(y * 10 + 10 + dz, 8)]
        return jnp.concatenate([lower, upper], axis=0).reshape(256, 512)

    def forward(yq, carry):
        pre = jnp.zeros((256, 256), F32)
        for k9 in range(9):
            pre = pre + mm(window(bf, 2 * yq + k9 // 3, k9 % 3), wf[k9])
        sig = 1.0 / (1.0 + jnp.exp(-pre))
        hidden = (pre * sig).astype(BF).reshape(2, 4, 2, 16, 256)
        grad = []
        for j in range(2):
            for k in range(2):
                hid[j, k, yq] = hidden[j, :, k].reshape(64, 256)
            pair = [gh[j, k, yq].reshape(4, 1, 16, 256) for k in range(2)]
            grad.append(jnp.concatenate(pair, axis=1).reshape(128, 256))
        grad = jnp.concatenate(grad, axis=0) * sig * (1.0 + pre * (1.0 - sig))
        gpt[yq] = grad.T.astype(BF)
        grad = grad.astype(BF).reshape(2, 8, 16, 256)
        for j in range(2):
            bg[pl.ds((2 * yq + j + 1) * 10 + 1, 8), :, 128:384] = grad[j]
        return carry

    lax.fori_loop(0, 4, forward, 0)

    for side in range(2):
        z = 8 if side == 0 else 1
        flat = jnp.concatenate([bg[y * 10 + z, :, 128:384] for y in range(1, 9)], axis=0)
        faces = permuted("send_gz", flat).reshape(4, 32, 256)
        ogz[side] = faces
        rgz[side, 5:9] = faces
    copies = halo_send(3, 2, lambda side, b: ogz[side, b], sgz, rgz)

    def grad_conv(part):
        for dz in range(3):
            first = jnp.zeros((256, 256), F32)
            second = jnp.zeros((256, 256), F32)
            for yq in range(4):
                rows = window(bf, 2 * yq + part, dz)
                first = first + mm(gpt[yq], rows[:, 0:256])
                second = second + mm(gpt[yq], rows[:, 256:512])
            taps = (
                first[0:128, 0:128] + first[128:256, 128:256],
                first[0:128, 128:256] + second[128:256, 0:128],
                second[0:128, 0:128] + second[128:256, 128:256],
            )
            for dx in range(3):
                slot = dx * 3 + dz
                dwf[part, slot // 6, slot % 6] = taps[dx].T

    def core_copy(part):
        return pltpu.make_async_remote_copy(
            src_ref=s1.at[part], dst_ref=r1.at[part], send_sem=cs.at[part], recv_sem=cr.at[part],
            device_id=in_space(sibling), device_id_type=MESH,
        )

    def core_send(part):
        s1[part] = dwf[part, 1 - core].reshape(768, 128).astype(BF)
        core_copy(part).start()

    def plane_copy(part, k):
        return pltpu.make_async_remote_copy(
            src_ref=s2.at[part, lax.rem(plane + k, N_PLANE)], dst_ref=r2.at[part, plane],
            send_sem=xs.at[part, k], recv_sem=xr.at[part, k],
            device_id=in_plane(k), device_id_type=MESH,
        )

    def each(low_k, high_k, act):
        def body(k, carry):
            act(k)
            return carry

        lax.fori_loop(low_k, high_k, body, 0)

    def plane_send(part):
        core_copy(part).wait_recv()
        mine = dwf[part, core].reshape(768, 128) + r1[part].astype(F32)
        s2[part] = mine.astype(BF).reshape(16, 48, 128)
        each(1, N_PLANE, lambda k: plane_copy(part, k).start())
        r2[part, plane] = s2[part, plane]

    def z_copy(part, k):
        return pltpu.make_async_remote_copy(
            src_ref=r3.at[part, zpos], dst_ref=r3.at[part, zpos],
            send_sem=zs.at[part, k], recv_sem=zr.at[part, k],
            device_id=in_z(k), device_id_type=MESH,
        )

    def z_send(part):
        each(1, N_PLANE, lambda k: plane_copy(part, k).wait_recv())
        total = r2[part, 0].astype(F32)
        for i in range(1, N_PLANE):
            total = total + r2[part, i].astype(F32)
        r3[part, zpos] = total.astype(BF)
        each(1, N_Z, lambda k: z_copy(part, k).start())

    def gather_copy(part, k):
        return pltpu.make_async_remote_copy(
            src_ref=fin.at[part], dst_ref=sums_o.at[part, core, plane],
            send_sem=as_.at[part, k], recv_sem=ar.at[part, k],
            device_id=in_plane(k), device_id_type=MESH,
        )

    def hand_copy(part, k):
        at = lax.rem(plane - k + N_PLANE, N_PLANE)
        return pltpu.make_async_remote_copy(
            src_ref=sums_o.at[part, core, at], dst_ref=sums_o.at[part, core, at],
            send_sem=fs.at[part, k], recv_sem=fr.at[part, k],
            device_id=in_space(sibling), device_id_type=MESH,
        )

    def gather_send(part):
        each(1, N_Z, lambda k: z_copy(part, k).wait_recv())
        total = r3[part, 0].astype(F32)
        for i in range(1, N_Z):
            total = total + r3[part, i].astype(F32)
        fin[part] = total.astype(BF)
        each(1, N_PLANE, lambda k: gather_copy(part, k).start())
        sums_o[part, core, plane] = fin[part]
        hand_copy(part, 0).start()

    def hand_over(part):
        def act(k):
            gather_copy(part, k).wait_recv()
            hand_copy(part, k).start()

        each(1, N_PLANE, act)

    def finish(part):
        each(0, N_PLANE, lambda k: hand_copy(part, k).wait_recv())
        core_copy(part).wait_send()
        each(1, N_PLANE, lambda k: plane_copy(part, k).wait_send())
        each(1, N_Z, lambda k: z_copy(part, k).wait_send())
        each(1, N_PLANE, lambda k: gather_copy(part, k).wait_send())
        each(0, N_PLANE, lambda k: hand_copy(part, k).wait_send())

    cot_t = cotp[...].astype(F32).T.astype(BF)
    for j in range(2):
        for k in range(2):
            out = mm(cot_t, hid[j, k].reshape(256, 256))
            for i in range(2):
                tap = 4 * i + 2 * j + k
                dwf[tap // 3, 1, 3 + tap % 3] = out[:, 128 * i : 128 * i + 128].T
    grad_conv(0)
    core_send(0)

    halo = halo_recv(2, copies, rgz)
    for side in range(2):
        z = 0 if side == 0 else 9
        out = permuted("recv_gz", jnp.concatenate(halo[side], axis=0))
        for y in range(8):
            bg[(y + 1) * 10 + z, :, 128:384] = out[16 * y : 16 * y + 16]

    for side in range(2):
        y = 8 if side == 0 else 1
        flat = bg[y * 10 : y * 10 + 10, :, 128:384].reshape(160, 256)
        flat = jnp.concatenate([flat, jnp.zeros((96, 256), BF)], axis=0)
        faces = permuted("send_gy", flat).reshape(4, 48, 256)
        ogy[side] = faces
        rgy[side, 5:9] = faces
    copies = halo_send(4, 1, lambda side, b: ogy[side, b], sgy, rgy)
    plane_send(0)
    grad_conv(1)
    core_send(1)
    halo = halo_recv(1, copies, rgy)
    for side in range(2):
        y = 0 if side == 0 else 9
        out = permuted("recv_gy", tall(halo[side], 64))
        put_rows(bg, y, 0, 10, slice(128, 384), out.reshape(10, 16, 256))

    for group in range(7):
        tiles = bg[16 * group : 16 * group + 16, :, 128:384].reshape(256, 256)
        out = permuted("send_gx", tiles)
        for b in range(4):
            rows = slice(16 * group, 16 * group + 16)
            for side in range(2):
                lanes = slice(128, 256) if side == 0 else slice(0, 128)
                face = out[64 * side + 16 * b : 64 * side + 16 * b + 16, lanes]
                ogx[side, b, rows] = face
                rgx[side, 5 + b, rows] = face
    copies = halo_send(5, 0, lambda side, b: ogx[side, b], sgx, rgx)
    plane_send(1)
    for group in range(7):
        at = slice(16 * group, 16 * group + 16)
        tiles = bg[at, :, 128:384].reshape(256, 256)
        bg[at, :, 0:128] = permuted("low", tiles[:, 128:256]).reshape(16, 16, 128)
        bg[at, :, 384:512] = permuted("high", tiles[:, 0:128]).reshape(16, 16, 128)
    grad_conv(2)
    core_send(2)

    total = jnp.zeros((256, 128), F32)
    for j in range(2):
        for k in range(2):
            total = total + mm(hid[j, k].reshape(256, 256), down_weight(j, k))
    out = permuted("swap", total.astype(BF))
    for b in range(4):
        for xq in range(4):
            at = 16 * (4 * xq + b)
            pooled_o[b, 16 * xq : 16 * xq + 16, :] = out[at : at + 16]

    halo = halo_recv(0, copies, rgx)
    for group in range(7):
        at = slice(16 * group, 16 * group + 16)
        rows = jnp.concatenate([halo[side][b][at] for side in range(2) for b in range(4)], axis=0)
        out = permuted("insert", rows)
        bg[at, :, 0:128] = bg[at, :, 0:128] + out[0:256].reshape(16, 16, 128)
        bg[at, :, 384:512] = bg[at, :, 384:512] + out[256:512].reshape(16, 16, 128)

    plane_send(2)
    z_send(0)

    def backward(yq, carry):
        grad = jnp.zeros((256, 256), F32)
        for k9 in range(9):
            grad = grad + mm_nt(window(bg, 2 * yq + k9 // 3, k9 % 3), wb[k9])
        out = permuted("swap", grad.astype(BF))
        for xq in range(4):
            for b in range(4):
                tile = out[16 * (4 * xq + b) : 16 * (4 * xq + b) + 16]
                for xl in range(2):
                    at = pl.ds(pl.multiple_of(64 * (2 * xq + xl) + 16 * yq, 16), 16)
                    dfeats_o[b, at, :] = tile[:, 128 * xl : 128 * xl + 128]
        return carry

    lax.fori_loop(0, 2, backward, 0)
    gather_send(0)
    z_send(1)
    lax.fori_loop(2, 4, backward, 0)
    gather_send(1)
    z_send(2)
    hand_over(0)
    gather_send(2)
    hand_over(1)
    hand_over(2)
    for one in sent:
        one.wait_send()
    for part in range(3):
        finish(part)


def per_device(feats, w_conv, w_down, cotangent, nbr_owner, nbr_slot):
    vmem = pl.BlockSpec(memory_space=pltpu.VMEM)
    smem = pl.BlockSpec(memory_space=pltpu.SMEM)
    anywhere = pl.BlockSpec(memory_space=pl.ANY)

    def buf(*shape, dtype=BF):
        return pltpu.VMEM(shape, dtype)

    def halo(rows, lanes, own=True):
        bufs = [buf(2, 4, rows, lanes), buf(2, 9, rows, lanes)]
        return ([buf(2, 4, rows, lanes)] if own else []) + bufs

    dma = pltpu.SemaphoreType.DMA
    pooled, d_feats, sums = pl.pallas_call(
        kernel,
        out_shape=(
            jax.ShapeDtypeStruct((4, 64, 128), BF),
            jax.ShapeDtypeStruct((4, 512, 128), BF),
            jax.ShapeDtypeStruct((3, 2, 16, 48, 128), BF),
        ),
        in_specs=[anywhere] * 5 + [smem] * 2,
        out_specs=(vmem, vmem, vmem),
        scratch_shapes=[
            buf(4, 512, 128), buf(27, 128, 128), buf(8, 128, 128), buf(4, 64, 128),
            buf(*TABLES.shape),
            buf(100, 16, 512), buf(112, 16, 512),
            buf(9, 512, 256), buf(9, 256, 512),
            buf(2, 2, 4, 64, 256, dtype=F32), buf(2, 2, 4, 64, 256),
            buf(4, 256, 256), buf(256, 128),
            buf(3, 2, 6, 128, 128, dtype=F32),
            *halo(64, 128, own=False), *halo(48, 256), *halo(64, 256),
            *halo(32, 256), *halo(48, 256), *halo(112, 128),
            buf(3, 768, 128), buf(3, 768, 128),
            buf(3, 16, 48, 128), buf(3, 16, 48, 128), buf(3, 8, 48, 128), buf(3, 48, 128),
            dma((5,)),
            dma((6, 2, 4)), dma((6, 2, 4)),
            dma((3,)), dma((3,)),
            dma((3, 16)), dma((3, 16)),
            dma((3, 8)), dma((3, 8)),
            dma((3, 16)), dma((3, 16)),
            dma((3, 16)), dma((3, 16)),
        ],
        compiler_params=pltpu.CompilerParams(
            collective_id=0, has_side_effects=True, vmem_limit_bytes=48 * 1024 * 1024
        ),
    )(
        feats[0], w_conv, w_down, cotangent[0], jnp.asarray(TABLES, BF), nbr_owner, nbr_slot
    )
    norm_factor = 1.0 / float(lax.axis_size("rep") * lax.axis_size("space") * 4 * 512) ** 0.5
    sums = sums.reshape(3, 12, 128, 128).astype(F32) * norm_factor
    grad_conv = sums[:, 0:9].reshape(3, 3, 3, 128, 128).transpose(1, 0, 2, 3, 4)
    grad_down = sums[:, 9:12].reshape(9, 128, 128)[0:8]
    return (pooled[None], d_feats[None], grad_conv.reshape(27, 128, 128), grad_down)


def solution(mesh):
    placed = (
        P("rep", "space", None, None),
        P(),
        P(),
        P("rep", "space", None, None),
        P("rep", "space", None),
        P("rep", "space", None),
    )
    return jax.shard_map(
        per_device,
        mesh=mesh,
        in_specs=placed,
        out_specs=(P("rep", "space", None, None), P("rep", "space", None, None), P(), P()),
        check_vma=False,
    )
```

```python
import functools

import jax
import jax.numpy as jnp
import numpy as np
from jax import lax
from jax.experimental import pallas as pl
from jax.experimental.pallas import tpu as pltpu
from jax.sharding import PartitionSpec as P

BF = jnp.bfloat16
F32 = jnp.float32
MESH = pl.DeviceIdType.MESH
SHIFTS = (-2, -1, 1, 2)
N_SPACE = 64
N_PLANE = 16
N_Z = 8


def onehot_tables():
    tables = {}

    def table(name, rows, cols):
        tables[name] = np.zeros((rows, cols), np.float32)
        return tables[name]

    swap = table("swap", 256, 256)
    for p in range(16):
        for q in range(16):
            swap[p * 16 + q, q * 16 + p] = 1
    send_y, recv_y = table("send_y", 192, 256), table("recv_y", 256, 256)
    send_z, recv_z = table("send_z", 256, 384), table("recv_z", 320, 256)
    send_gz, recv_gz = table("send_gz", 128, 128), table("recv_gz", 128, 128)
    send_gy, recv_gy = table("send_gy", 192, 256), table("recv_gy", 160, 256)
    send_gx = table("send_gx", 128, 256)
    low, high = table("low", 256, 256), table("high", 256, 256)
    insert = table("insert", 512, 128)
    for b in range(4):
        for xq in range(4):
            row = xq * 4 + b
            for z in range(8):
                send_y[b * 48 + xq * 8 + z, z * 16 + row] = 1
                recv_y[z * 16 + row, b * 64 + xq * 8 + z] = 1
                far = (xq + 1) * 8 + z if xq < 3 else 40 + z
                recv_y[128 + z * 16 + row, b * 64 + far] = 1
                if xq == 3:
                    send_y[b * 48 + 40 + z, 128 + z * 16 + row] = 1
                send_gz[b * 32 + z * 4 + xq, z * 16 + row] = 1
                recv_gz[z * 16 + row, b * 32 + z * 4 + xq] = 1
            for y in range(10):
                send_z[b * 64 + xq * 10 + y, y * 16 + row] = 1
                recv_z[y * 16 + row, b * 64 + xq * 10 + y] = 1
                far = (xq + 1) * 10 + y if xq < 3 else 40 + y
                recv_z[160 + y * 16 + row, b * 64 + far] = 1
                if xq == 3:
                    send_z[b * 64 + 40 + y, 160 + y * 16 + row] = 1
                send_gy[b * 48 + y * 4 + xq, y * 16 + row] = 1
                recv_gy[y * 16 + row, b * 64 + y * 4 + xq] = 1
            for k in range(16):
                if xq >= 1:
                    low[k * 16 + row, k * 16 + row - 4] = 1
                if xq <= 2:
                    high[k * 16 + row, k * 16 + row + 4] = 1
        for k in range(16):
            send_gx[b * 16 + k, k * 16 + 12 + b] = 1
            send_gx[64 + b * 16 + k, k * 16 + b] = 1
            insert[k * 16 + b, b * 16 + k] = 1
            insert[256 + k * 16 + 12 + b, 64 + b * 16 + k] = 1
    places, parts, start = {}, [], 0
    for name, value in tables.items():
        rows, cols = value.shape
        places[name] = (start, rows, cols)
        parts.append(np.pad(value, ((0, 0), (0, 384 - cols))))
        start += rows
    return places, np.concatenate(parts)


PLACES, TABLES = onehot_tables()


def mm(left, right):
    return jnp.dot(left, right, preferred_element_type=F32)


def mm_nt(left, right):
    return lax.dot_general(left, right, (((1,), (1,)), ((), ())), preferred_element_type=F32)


def kernel(
    feats_h, wc_h, wd_h, cot_h, tab_h, own_h, slot_h,
    pooled_o, dfeats_o, sums_o,
    feats, wc, wd, cot, tab, own_s, slot_s, bf, bg, wf, wb, gh, hid, gpt, cotp, dwf,
    sx, rx, oy, sy, ry, oz, sz, rz, ogz, sgz, rgz, ogy, sgy, rgy, ogx, sgx, rgx,
    s1, r1, s2, r2, r3, fin,
    lsem, hs, hr, cs, cr, xs, xr, zs, zr, as_, ar, fs, fr,
):
    pos = lax.axis_index("space")
    rep = lax.axis_index("rep")
    core = lax.rem(pos, 2)
    zpos = lax.rem(lax.div(pos, 2), 8)
    xpos = lax.div(pos, 16)
    plane = xpos * 4 + rep
    sibling = pos + 1 - 2 * core

    def in_space(to):
        return {"space": to, "rep": rep}

    def in_plane(k):
        to = lax.rem(plane + k, N_PLANE)
        return {"space": lax.div(to, 4) * 16 + lax.rem(pos, 16), "rep": lax.rem(to, 4)}

    def in_z(k):
        to = lax.rem(zpos + k, N_Z)
        return {"space": xpos * 16 + to * 2 + core, "rep": rep}

    loads = [
        pltpu.make_async_copy(src, dst, lsem.at[i])
        for i, (src, dst) in enumerate(
            (
                (own_h, own_s), (slot_h, slot_s), (feats_h, feats), (tab_h, tab),
                (cot_h, cot), (wc_h, wc), (wd_h, wd),
            )
        )
    ]
    for one in loads:
        one.start()

    barrier = pltpu.get_barrier_semaphore()
    for t in SHIFTS:
        to = lax.rem(pos + t + N_SPACE, N_SPACE)
        pl.semaphore_signal(barrier, inc=1, device_id=in_space(to), device_id_type=MESH)
    pl.semaphore_signal(barrier, inc=1, device_id=in_space(sibling), device_id_type=MESH)

    def greet_plane(k, carry):
        pl.semaphore_signal(barrier, inc=1, device_id=in_plane(k), device_id_type=MESH)
        return carry

    def greet_z(k, carry):
        pl.semaphore_signal(barrier, inc=1, device_id=in_z(k), device_id_type=MESH)
        return carry

    lax.fori_loop(1, N_PLANE, greet_plane, 0)
    lax.fori_loop(1, N_Z, greet_z, 0)

    loads[0].wait()
    loads[1].wait()

    owners = [[own_s[0, b, d] for d in range(6)] for b in range(4)]
    slots = [[slot_s[0, b, d] for d in range(6)] for b in range(4)]

    def pick(d, t):
        found = jnp.int32(0)
        for b in range(1, 4):
            hit = (owners[b][d] == pos + t) & (owners[b][d] >= 0)
            found = jnp.where(hit, b, found)
        return found

    def place(d, b):
        gap = pos - owners[b][d]
        far = jnp.clip(jnp.where(gap < 0, gap + 2, gap + 1), 0, 3)
        near = jnp.clip(5 + slots[b][d], 5, 8)
        return jnp.where(owners[b][d] < 0, 4, jnp.where(gap == 0, near, far))

    for ref in (rx, ry, rz, rgz, rgy, rgx):
        ref[4] = jnp.zeros(ref.shape[1:], BF)

    def halo_copy(phase, i, send, recv):
        to = lax.rem(pos + SHIFTS[i] + N_SPACE, N_SPACE)
        return pltpu.make_async_remote_copy(
            src_ref=send.at[i],
            dst_ref=recv.at[i],
            send_sem=hs.at[phase, i],
            recv_sem=hr.at[phase, i],
            device_id=in_space(to),
            device_id_type=MESH,
        )

    sent = []

    def halo_send(phase, axis, own, send, recv):
        copies = []
        for i, t in enumerate(SHIFTS):
            for side in range(2):
                send[i, side] = own(side, pick(2 * axis + side, t))
            one = halo_copy(phase, i, send, recv)
            one.start()
            copies.append(one)
        sent.extend(copies)
        return copies

    def halo_recv(axis, copies, recv):
        for one in copies:
            one.wait_recv()
        return [
            [recv[place(2 * axis + 1 - side, b), side] for b in range(4)] for side in range(2)
        ]

    def onehot(name):
        start, rows, cols = PLACES[name]
        return tab[start : start + rows, 0:cols]

    def permuted(name, value):
        return mm(onehot(name), value).astype(BF)

    loads[2].wait()
    for b in range(4):
        rx[5 + b, 0] = feats[b, 448:512, :]
        rx[5 + b, 1] = feats[b, 0:64, :]
    for side in range(2):
        for i, t in enumerate(SHIFTS):
            rows = slice(448, 512) if side == 0 else slice(0, 64)
            sx[i, side] = feats[pick(side, t), rows, :]
    pl.semaphore_wait(barrier, 4 + 1 + N_PLANE - 1 + N_Z - 1)
    copies = [halo_copy(0, i, sx, rx) for i in range(4)]
    for one in copies:
        one.start()
    sent.extend(copies)

    loads[3].wait()

    def x_layer(s, chunk, halo):
        rows = []
        for xq in range(4):
            x = 2 * xq + s - 1
            for b in range(4):
                if x < 0 or x > 7:
                    rows.append(halo[0 if x < 0 else 1][b][16 * chunk : 16 * chunk + 16])
                else:
                    rows.append(feats[b, 64 * x + 16 * chunk : 64 * x + 16 * chunk + 16, :])
        return jnp.concatenate(rows, axis=0)

    def put_rows(ref, y, z, count, lanes, value):
        ref[pl.ds(y * 10 + z, count), :, lanes] = value

    for chunk in range(4):
        both = jnp.concatenate([x_layer(1, chunk, None), x_layer(2, chunk, None)], axis=1)
        out = permuted("swap", both).reshape(2, 8, 16, 256)
        for j in range(2):
            put_rows(bf, 2 * chunk + j + 1, 1, 8, slice(128, 384), out[j])

    halo = halo_recv(0, copies, rx)
    for chunk in range(4):
        both = jnp.concatenate([x_layer(0, chunk, halo), x_layer(3, chunk, halo)], axis=1)
        out = permuted("swap", both).reshape(2, 8, 16, 256)
        for j in range(2):
            put_rows(bf, 2 * chunk + j + 1, 1, 8, slice(0, 128), out[j, :, :, 0:128])
            put_rows(bf, 2 * chunk + j + 1, 1, 8, slice(384, 512), out[j, :, :, 128:256])

    for side in range(2):
        y = 8 if side == 0 else 1
        layer = bf[y * 10 + 1 : y * 10 + 9].reshape(128, 512)
        flat = jnp.concatenate([layer[:, 0:256], layer[:, 256:512]], axis=0)
        faces = permuted("send_y", flat).reshape(4, 48, 256)
        oy[side] = faces
        ry[5:9, side] = faces
    copies = halo_send(1, 1, lambda side, b: oy[side, b], sy, ry)

    for one in loads[4:]:
        one.wait()
    cot_rows = jnp.concatenate(
        [cot[b, 16 * xq : 16 * xq + 16, :] for xq in range(4) for b in range(4)], axis=0
    )
    cot_perm = permuted("swap", cot_rows)
    cotp[...] = cot_perm

    def down_weight(j, k):
        return jnp.concatenate([wd[2 * j + k], wd[4 + 2 * j + k]], axis=0)

    for j in range(2):
        for k in range(2):
            out = mm_nt(cot_perm, down_weight(j, k)).reshape(4, 4, 16, 256)
            for zq in range(4):
                gh[j, 2 * zq + k] = out[:, zq]

    def weights(k9, carry):
        for s in range(4):
            for xl in range(2):
                dx = s - xl
                fwd_at = (pl.ds(s * 128, 128), pl.ds(xl * 128, 128))
                bwd_at = (pl.ds(xl * 128, 128), pl.ds(s * 128, 128))
                if 0 <= dx <= 2:
                    wf[(k9,) + fwd_at] = wc[9 * dx + k9]
                    wb[(k9,) + bwd_at] = wc[9 * (2 - dx) + 8 - k9]
                else:
                    wf[(k9,) + fwd_at] = jnp.zeros((128, 128), BF)
                    wb[(k9,) + bwd_at] = jnp.zeros((128, 128), BF)
        return carry

    lax.fori_loop(0, 9, weights, 0)

    def tall(values, rows):
        pad = jnp.zeros((rows - values[0].shape[0], values[0].shape[1]), BF)
        return jnp.concatenate([v for value in values for v in (value, pad)], axis=0)

    halo = halo_recv(1, copies, ry)
    for side in range(2):
        y = 0 if side == 0 else 9
        out = permuted("recv_y", tall(halo[side], 64))
        put_rows(bf, y, 1, 8, slice(0, 256), out[0:128].reshape(8, 16, 256))
        put_rows(bf, y, 1, 8, slice(256, 512), out[128:256].reshape(8, 16, 256))

    for side in range(2):
        z = 8 if side == 0 else 1
        near = [bf[y * 10 + z, :, 0:256] for y in range(10)]
        far = [bf[y * 10 + z, :, 256:512] for y in range(10)]
        flat = jnp.concatenate(near + far + [jnp.zeros((64, 256), BF)], axis=0)
        faces = permuted("send_z", flat).reshape(4, 64, 256)
        oz[side] = faces
        rz[5:9, side] = faces
    copies = halo_send(2, 2, lambda side, b: oz[side, b], sz, rz)
    bg[100:112] = jnp.zeros((12, 16, 512), BF)
    dwf[2, 1, 5] = jnp.zeros((128, 128), F32)
    def window(ref, y, z, count):
        lower = ref[pl.ds(y * 10 + z, count)]
        upper = ref[pl.ds(y * 10 + 10 + z, count)]
        return jnp.concatenate([lower, upper], axis=0).reshape(32 * count, 512)

    def activate(pre, grad):
        sig = 1.0 / (1.0 + jnp.exp(-pre))
        hidden = (pre * sig).astype(BF).reshape(-1, 16, 256)
        grad = (grad * sig * (1.0 + pre * (1.0 - sig))).astype(BF)
        return hidden, grad.reshape(-1, 16, 256)

    def inner(yq, carry):
        pre = jnp.zeros((192, 256), F32)
        for k9 in range(9):
            pre = pre + mm(window(bf, 2 * yq + k9 // 3, 1 + k9 % 3, 6), wf[k9])
        grad = jnp.concatenate([gh[j, 1:7, yq] for j in range(2)], axis=0).reshape(192, 256)
        hidden, grad = activate(pre, grad)
        for j in range(2):
            hid[j, 1:7, yq] = hidden[6 * j : 6 * j + 6]
            bg[pl.ds((2 * yq + j + 1) * 10 + 2, 6), :, 128:384] = grad[6 * j : 6 * j + 6]
        return carry

    lax.fori_loop(0, 4, inner, 0)

    halo = halo_recv(2, copies, rz)
    for side in range(2):
        z = 0 if side == 0 else 9
        out = permuted("recv_z", jnp.concatenate(halo[side], axis=0))
        for y in range(10):
            bf[y * 10 + z, :, 0:256] = out[16 * y : 16 * y + 16]
            bf[y * 10 + z, :, 256:512] = out[160 + 16 * y : 160 + 16 * y + 16]

    outer = [(y, z) for y in range(8) for z in (0, 7)]
    pre = jnp.zeros((256, 256), F32)
    for k9 in range(9):
        tiles = [bf[(y + k9 // 3) * 10 + z + k9 % 3] for y, z in outer]
        pre = pre + mm(jnp.concatenate(tiles, axis=0), wf[k9])
    grad = jnp.concatenate([gh[y % 2, z, y // 2] for y, z in outer], axis=0)
    hidden, grad = activate(pre, grad)
    for at, (y, z) in enumerate(outer):
        hid[y % 2, z, y // 2] = hidden[at]
        bg[(y + 1) * 10 + z + 1, :, 128:384] = grad[at]

    for side in range(2):
        z = 8 if side == 0 else 1
        flat = jnp.concatenate([bg[y * 10 + z, :, 128:384] for y in range(1, 9)], axis=0)
        faces = permuted("send_gz", flat).reshape(4, 32, 256)
        ogz[side] = faces
        rgz[5:9, side] = faces
    copies = halo_send(3, 2, lambda side, b: ogz[side, b], sgz, rgz)

    def grad_conv(part):
        for dz in range(3):
            first = jnp.zeros((256, 256), F32)
            second = jnp.zeros((256, 256), F32)
            for yq in range(4):
                rows = window(bf, 2 * yq + part, dz, 8)
                first = first + mm(gpt[yq], rows[:, 0:256])
                second = second + mm(gpt[yq], rows[:, 256:512])
            taps = (
                first[0:128, 0:128] + first[128:256, 128:256],
                first[0:128, 128:256] + second[128:256, 0:128],
                second[0:128, 0:128] + second[128:256, 128:256],
            )
            for dx in range(3):
                slot = dx * 3 + dz
                dwf[part, slot // 6, slot % 6] = taps[dx].T

    def core_copy(part):
        return pltpu.make_async_remote_copy(
            src_ref=s1.at[part], dst_ref=r1.at[part], send_sem=cs.at[part], recv_sem=cr.at[part],
            device_id=in_space(sibling), device_id_type=MESH,
        )

    def core_send(part):
        s1[part] = dwf[part, 1 - core].reshape(768, 128).astype(BF)
        core_copy(part).start()

    def plane_copy(part, k):
        return pltpu.make_async_remote_copy(
            src_ref=s2.at[part, lax.rem(plane + k, N_PLANE)], dst_ref=r2.at[part, plane],
            send_sem=xs.at[part], recv_sem=xr.at[part],
            device_id=in_plane(k), device_id_type=MESH,
        )

    def each(low_k, high_k, act):
        def body(k, carry):
            act(k)
            return carry

        lax.fori_loop(low_k, high_k, body, 0)

    def plane_send(part):
        core_copy(part).wait_recv()
        mine = dwf[part, core].reshape(768, 128) + r1[part].astype(F32)
        s2[part] = mine.astype(BF).reshape(16, 48, 128)
        each(1, N_PLANE, lambda k: plane_copy(part, k).start())
        r2[part, plane] = s2[part, plane]

    def z_copy(part, k):
        return pltpu.make_async_remote_copy(
            src_ref=r3.at[part, zpos], dst_ref=r3.at[part, zpos],
            send_sem=zs.at[part], recv_sem=zr.at[part],
            device_id=in_z(k), device_id_type=MESH,
        )

    def z_send(part):
        all_bytes(r2.at[part, 0 : N_PLANE - 1], xr.at[part])
        total = r2[part, 0].astype(F32)
        for i in range(1, N_PLANE):
            total = total + r2[part, i].astype(F32)
        r3[part, zpos] = total.astype(BF)
        each(1, N_Z, lambda k: z_copy(part, k).start())

    def gather_copy(part, k):
        return pltpu.make_async_remote_copy(
            src_ref=fin.at[part], dst_ref=sums_o.at[part, core, plane],
            send_sem=as_.at[part], recv_sem=ar.at[part],
            device_id=in_plane(k), device_id_type=MESH,
        )

    def hand_copy(part):
        half = sums_o.at[part, core]
        return pltpu.make_async_remote_copy(
            src_ref=half, dst_ref=half, send_sem=fs.at[part], recv_sem=fr.at[part],
            device_id=in_space(sibling), device_id_type=MESH,
        )

    def all_bytes(ref, sem):
        pltpu.make_async_copy(ref, ref, sem).wait()

    def gather_send(part):
        all_bytes(r3.at[part, 0 : N_Z - 1], zr.at[part])
        total = r3[part, 0].astype(F32)
        for i in range(1, N_Z):
            total = total + r3[part, i].astype(F32)
        fin[part] = total.astype(BF)
        each(1, N_PLANE, lambda k: gather_copy(part, k).start())
        sums_o[part, core, plane] = fin[part]

    def hand_over(part):
        all_bytes(sums_o.at[part, core, 0 : N_PLANE - 1], ar.at[part])
        hand_copy(part).start()

    def finish(part):
        hand_copy(part).wait_recv()
        core_copy(part).wait_send()
        all_bytes(s2.at[part, 0 : N_PLANE - 1], xs.at[part])
        all_bytes(r3.at[part, 0 : N_Z - 1], zs.at[part])
        all_bytes(sums_o.at[part, core, 0 : N_PLANE - 1], as_.at[part])
        hand_copy(part).wait_send()

    def down_rows(j, k):
        tiles = [hid[j, 2 * zq + k, yq] for yq in range(4) for zq in range(4)]
        return jnp.concatenate(tiles, axis=0)

    for yq in range(4):
        gpt[yq] = window(bg, 2 * yq + 1, 1, 8)[:, 128:384].astype(F32).T.astype(BF)
    cot_t = cotp[...].astype(F32).T.astype(BF)
    for j in range(2):
        for k in range(2):
            out = mm(cot_t, down_rows(j, k))
            for i in range(2):
                tap = 4 * i + 2 * j + k
                dwf[tap // 3, 1, 3 + tap % 3] = out[:, 128 * i : 128 * i + 128].T
    grad_conv(0)
    core_send(0)
    grad_conv(1)
    core_send(1)
    plane_send(0)

    halo = halo_recv(2, copies, rgz)
    for side in range(2):
        z = 0 if side == 0 else 9
        out = permuted("recv_gz", jnp.concatenate(halo[side], axis=0))
        for y in range(8):
            bg[(y + 1) * 10 + z, :, 128:384] = out[16 * y : 16 * y + 16]

    for side in range(2):
        y = 8 if side == 0 else 1
        flat = bg[y * 10 : y * 10 + 10, :, 128:384].reshape(160, 256)
        flat = jnp.concatenate([flat, jnp.zeros((96, 256), BF)], axis=0)
        faces = permuted("send_gy", flat).reshape(4, 48, 256)
        ogy[side] = faces
        rgy[5:9, side] = faces
    copies = halo_send(4, 1, lambda side, b: ogy[side, b], sgy, rgy)
    grad_conv(2)
    core_send(2)
    plane_send(1)
    plane_send(2)
    halo = halo_recv(1, copies, rgy)
    for side in range(2):
        y = 0 if side == 0 else 9
        out = permuted("recv_gy", tall(halo[side], 64))
        put_rows(bg, y, 0, 10, slice(128, 384), out.reshape(10, 16, 256))

    for group in range(7):
        tiles = bg[16 * group : 16 * group + 16, :, 128:384].reshape(256, 256)
        out = permuted("send_gx", tiles)
        for b in range(4):
            rows = slice(16 * group, 16 * group + 16)
            for side in range(2):
                lanes = slice(128, 256) if side == 0 else slice(0, 128)
                face = out[64 * side + 16 * b : 64 * side + 16 * b + 16, lanes]
                ogx[side, b, rows] = face
                rgx[5 + b, side, rows] = face
    copies = halo_send(5, 0, lambda side, b: ogx[side, b], sgx, rgx)
    for group in range(7):
        at = slice(16 * group, 16 * group + 16)
        tiles = bg[at, :, 128:384].reshape(256, 256)
        bg[at, :, 0:128] = permuted("low", tiles[:, 128:256]).reshape(16, 16, 128)
        bg[at, :, 384:512] = permuted("high", tiles[:, 0:128]).reshape(16, 16, 128)
    z_send(0)

    total = jnp.zeros((256, 128), F32)
    for j in range(2):
        for k in range(2):
            total = total + mm(down_rows(j, k), down_weight(j, k))
    out = permuted("swap", total.astype(BF))
    for b in range(4):
        for xq in range(4):
            at = 16 * (4 * xq + b)
            pooled_o[b, 16 * xq : 16 * xq + 16, :] = out[at : at + 16]

    halo = halo_recv(0, copies, rgx)
    for group in range(7):
        at = slice(16 * group, 16 * group + 16)
        rows = jnp.concatenate([halo[side][b][at] for side in range(2) for b in range(4)], axis=0)
        out = permuted("insert", rows)
        bg[at, :, 0:128] = bg[at, :, 0:128] + out[0:256].reshape(16, 16, 128)
        bg[at, :, 384:512] = bg[at, :, 384:512] + out[256:512].reshape(16, 16, 128)

    z_send(1)
    z_send(2)

    def backward(yq, carry):
        grad = jnp.zeros((256, 256), F32)
        for k9 in range(9):
            grad = grad + mm_nt(window(bg, 2 * yq + k9 // 3, k9 % 3, 8), wb[k9])
        out = permuted("swap", grad.astype(BF))
        for xq in range(4):
            for b in range(4):
                tile = out[16 * (4 * xq + b) : 16 * (4 * xq + b) + 16]
                for xl in range(2):
                    at = pl.ds(pl.multiple_of(64 * (2 * xq + xl) + 16 * yq, 16), 16)
                    dfeats_o[b, at, :] = tile[:, 128 * xl : 128 * xl + 128]
        return carry

    lax.fori_loop(0, 2, backward, 0)
    gather_send(0)
    gather_send(1)
    gather_send(2)
    lax.fori_loop(2, 4, backward, 0)
    hand_over(0)
    hand_over(1)
    hand_over(2)
    for one in sent:
        one.wait_send()
    for part in range(3):
        finish(part)


def epilogue(norm, sums, pooled, dfeats, pooled_o, dfeats_o, conv_o, down_o, conv, down, sem):
    copies = [
        pltpu.make_async_copy(dfeats, dfeats_o, sem.at[0]),
        pltpu.make_async_copy(pooled, pooled_o, sem.at[1]),
    ]
    copies[0].start()
    copies[1].start()
    for part in range(3):
        conv[part] = (sums[part, 0:9].astype(F32) * norm).reshape(3, 3, 128, 128)
        one = pltpu.make_async_copy(conv.at[part], conv_o.at[:, part], sem.at[2 + part])
        one.start()
        copies.append(one)
    for tap in range(8):
        down[tap] = sums[tap // 3, 9 + tap % 3].astype(F32) * norm
    one = pltpu.make_async_copy(down, down_o, sem.at[5])
    one.start()
    copies.append(one)
    for one in copies:
        one.wait()


def per_device(feats, w_conv, w_down, cotangent, nbr_owner, nbr_slot):
    def buf(*shape, dtype=BF):
        return pltpu.VMEM(shape, dtype)

    def halo(rows, lanes, own=True):
        bufs = [buf(4, 2, rows, lanes), buf(9, 2, rows, lanes)]
        return ([buf(2, 4, rows, lanes)] if own else []) + bufs

    def in_hbm(value):
        return pltpu.with_memory_space_constraint(value, pltpu.HBM)

    vmem = pl.BlockSpec(memory_space=pltpu.VMEM)
    hbm = pl.BlockSpec(memory_space=pltpu.HBM)
    dma = pltpu.SemaphoreType.DMA
    operands = (
        feats[0], w_conv, w_down, cotangent[0], jnp.asarray(TABLES, BF), nbr_owner, nbr_slot
    )
    pooled, d_feats, sums = pl.pallas_call(
        kernel,
        out_shape=(
            pltpu.VMEM((4, 64, 128), BF),
            pltpu.VMEM((4, 512, 128), BF),
            pltpu.VMEM((3, 2, 16, 48, 128), BF),
        ),
        in_specs=[hbm] * 7,
        out_specs=(vmem, vmem, vmem),
        scratch_shapes=[
            buf(4, 512, 128), buf(27, 128, 128), buf(8, 128, 128), buf(4, 64, 128),
            buf(*TABLES.shape),
            pltpu.SMEM((1, 4, 6), jnp.int32), pltpu.SMEM((1, 4, 6), jnp.int32),
            buf(100, 16, 512), buf(112, 16, 512),
            buf(9, 512, 256), buf(9, 256, 512),
            buf(2, 8, 4, 16, 256, dtype=F32), buf(2, 8, 4, 16, 256),
            buf(4, 256, 256), buf(256, 128),
            buf(3, 2, 6, 128, 128, dtype=F32),
            *halo(64, 128, own=False), *halo(48, 256), *halo(64, 256),
            *halo(32, 256), *halo(48, 256), *halo(112, 128),
            buf(3, 768, 128), buf(3, 768, 128),
            buf(3, 16, 48, 128), buf(3, 16, 48, 128), buf(3, 8, 48, 128), buf(3, 48, 128),
            dma((7,)),
            dma((6, 4)), dma((6, 4)),
            *([dma((3,))] * 10),
        ],
        compiler_params=pltpu.CompilerParams(
            collective_id=0, has_side_effects=True, vmem_limit_bytes=48 * 1024 * 1024
        ),
    )(*[in_hbm(one) for one in operands])
    norm = 1.0 / float(lax.axis_size("rep") * lax.axis_size("space") * 4 * 512) ** 0.5
    pooled, d_feats, conv, down = pl.pallas_call(
        functools.partial(epilogue, norm),
        out_shape=(
            jax.ShapeDtypeStruct((4, 64, 128), BF),
            jax.ShapeDtypeStruct((4, 512, 128), BF),
            jax.ShapeDtypeStruct((3, 3, 3, 128, 128), F32),
            jax.ShapeDtypeStruct((8, 128, 128), F32),
        ),
        in_specs=[vmem] * 3,
        out_specs=[hbm] * 4,
        scratch_shapes=[buf(3, 3, 3, 128, 128, dtype=F32), buf(8, 128, 128, dtype=F32), dma((6,))],
        compiler_params=pltpu.CompilerParams(vmem_limit_bytes=24 * 1024 * 1024),
    )(sums.reshape(3, 12, 128, 128), pooled, d_feats)
    return (pooled[None], d_feats[None], conv.reshape(27, 128, 128), down)


def solution(mesh):
    placed = (
        P("rep", "space", None, None),
        P(),
        P(),
        P("rep", "space", None, None),
        P("rep", "space", None),
        P("rep", "space", None),
    )
    return jax.shard_map(
        per_device,
        mesh=mesh,
        in_specs=placed,
        out_specs=(P("rep", "space", None, None), P("rep", "space", None, None), P(), P()),
        check_vma=False,
    )
```

```python
import functools

import jax
import jax.numpy as jnp
import numpy as np
from jax import lax
from jax.experimental import pallas as pl
from jax.experimental.pallas import tpu as pltpu
from jax.sharding import PartitionSpec as P

BF = jnp.bfloat16
F32 = jnp.float32
MESH = pl.DeviceIdType.MESH
SHIFTS = (-2, -1, 1, 2)
N_SPACE = 64
N_PLANE = 16
N_Z = 8


def onehot_tables():
    tables = {}

    def table(name, rows, cols):
        tables[name] = np.zeros((rows, cols), np.float32)
        return tables[name]

    swap = table("swap", 256, 256)
    for p in range(16):
        for q in range(16):
            swap[p * 16 + q, q * 16 + p] = 1
    send_y, recv_y = table("send_y", 192, 256), table("recv_y", 256, 256)
    send_z, recv_z = table("send_z", 256, 384), table("recv_z", 320, 256)
    send_gz, recv_gz = table("send_gz", 128, 128), table("recv_gz", 128, 128)
    send_gy, recv_gy = table("send_gy", 192, 256), table("recv_gy", 160, 256)
    send_gx = table("send_gx", 128, 256)
    low, high = table("low", 256, 256), table("high", 256, 256)
    insert = table("insert", 512, 128)
    for b in range(4):
        for xq in range(4):
            row = xq * 4 + b
            for z in range(8):
                send_y[b * 48 + xq * 8 + z, z * 16 + row] = 1
                recv_y[z * 16 + row, b * 64 + xq * 8 + z] = 1
                far = (xq + 1) * 8 + z if xq < 3 else 40 + z
                recv_y[128 + z * 16 + row, b * 64 + far] = 1
                if xq == 3:
                    send_y[b * 48 + 40 + z, 128 + z * 16 + row] = 1
                send_gz[b * 32 + z * 4 + xq, z * 16 + row] = 1
                recv_gz[z * 16 + row, b * 32 + z * 4 + xq] = 1
            for y in range(10):
                send_z[b * 64 + xq * 10 + y, y * 16 + row] = 1
                recv_z[y * 16 + row, b * 64 + xq * 10 + y] = 1
                far = (xq + 1) * 10 + y if xq < 3 else 40 + y
                recv_z[160 + y * 16 + row, b * 64 + far] = 1
                if xq == 3:
                    send_z[b * 64 + 40 + y, 160 + y * 16 + row] = 1
                send_gy[b * 48 + y * 4 + xq, y * 16 + row] = 1
                recv_gy[y * 16 + row, b * 64 + y * 4 + xq] = 1
            for k in range(16):
                if xq >= 1:
                    low[k * 16 + row, k * 16 + row - 4] = 1
                if xq <= 2:
                    high[k * 16 + row, k * 16 + row + 4] = 1
        for k in range(16):
            send_gx[b * 16 + k, k * 16 + 12 + b] = 1
            send_gx[64 + b * 16 + k, k * 16 + b] = 1
            insert[k * 16 + b, b * 16 + k] = 1
            insert[256 + k * 16 + 12 + b, 64 + b * 16 + k] = 1
    places, parts, start = {}, [], 0
    for name, value in tables.items():
        rows, cols = value.shape
        places[name] = (start, rows, cols)
        parts.append(np.pad(value, ((0, 0), (0, 384 - cols))))
        start += rows
    return places, np.concatenate(parts)


PLACES, TABLES = onehot_tables()


def mm(left, right):
    return jnp.dot(left, right, preferred_element_type=F32)


def mm_nt(left, right):
    return lax.dot_general(left, right, (((1,), (1,)), ((), ())), preferred_element_type=F32)


def kernel(
    feats_h, wc_h, wd_h, cot_h, tab_h, own_h, slot_h,
    pooled_o, dfeats_o, sums_o,
    feats, wc, wd, cot, tab, own_s, slot_s, bf, bg, wf, wb, gh, hid, gpt, cotp, dwf,
    sx, rx, oy, sy, ry, oz, sz, rz, ogz, sgz, rgz, ogy, sgy, rgy, ogx, sgx, rgx,
    s1, r1, s2, r2, r3, fin,
    lsem, hs, hr, cs, cr, xs, xr, zs, zr, as_, ar, fs, fr,
):
    pos = lax.axis_index("space")
    rep = lax.axis_index("rep")
    core = lax.rem(pos, 2)
    zpos = lax.rem(lax.div(pos, 2), 8)
    xpos = lax.div(pos, 16)
    plane = xpos * 4 + rep
    sibling = pos + 1 - 2 * core

    def in_space(to):
        return {"space": to, "rep": rep}

    def in_plane(k):
        to = lax.rem(plane + k, N_PLANE)
        return {"space": lax.div(to, 4) * 16 + lax.rem(pos, 16), "rep": lax.rem(to, 4)}

    def in_z(k):
        to = lax.rem(zpos + k, N_Z)
        return {"space": xpos * 16 + to * 2 + core, "rep": rep}

    loads = [
        pltpu.make_async_copy(src, dst, lsem.at[i])
        for i, (src, dst) in enumerate(
            (
                (own_h, own_s), (slot_h, slot_s), (feats_h, feats), (tab_h, tab),
                (cot_h, cot), (wc_h, wc), (wd_h, wd),
            )
        )
    ]
    for one in loads:
        one.start()

    barrier = pltpu.get_barrier_semaphore()
    for t in SHIFTS:
        to = lax.rem(pos + t + N_SPACE, N_SPACE)
        pl.semaphore_signal(barrier, inc=1, device_id=in_space(to), device_id_type=MESH)
    pl.semaphore_signal(barrier, inc=1, device_id=in_space(sibling), device_id_type=MESH)

    def greet_plane(k, carry):
        pl.semaphore_signal(barrier, inc=1, device_id=in_plane(k), device_id_type=MESH)
        return carry

    def greet_z(k, carry):
        pl.semaphore_signal(barrier, inc=1, device_id=in_z(k), device_id_type=MESH)
        return carry

    lax.fori_loop(1, N_PLANE, greet_plane, 0)
    lax.fori_loop(1, N_Z, greet_z, 0)

    loads[0].wait()
    loads[1].wait()

    owners = [[own_s[0, b, d] for d in range(6)] for b in range(4)]
    slots = [[slot_s[0, b, d] for d in range(6)] for b in range(4)]

    def pick(d, t):
        found = jnp.int32(0)
        for b in range(1, 4):
            hit = (owners[b][d] == pos + t) & (owners[b][d] >= 0)
            found = jnp.where(hit, b, found)
        return found

    def place(d, b):
        gap = pos - owners[b][d]
        far = jnp.clip(jnp.where(gap < 0, gap + 2, gap + 1), 0, 3)
        near = jnp.clip(5 + slots[b][d], 5, 8)
        return jnp.where(owners[b][d] < 0, 4, jnp.where(gap == 0, near, far))

    for ref in (rx, ry, rz, rgz, rgy, rgx):
        ref[4] = jnp.zeros(ref.shape[1:], BF)

    def halo_copy(phase, i, send, recv):
        to = lax.rem(pos + SHIFTS[i] + N_SPACE, N_SPACE)
        return pltpu.make_async_remote_copy(
            src_ref=send.at[i],
            dst_ref=recv.at[i],
            send_sem=hs.at[phase, i],
            recv_sem=hr.at[phase, i],
            device_id=in_space(to),
            device_id_type=MESH,
        )

    sent = []

    def halo_send(phase, axis, own, send, recv):
        copies = []
        for i, t in enumerate(SHIFTS):
            for side in range(2):
                send[i, side] = own(side, pick(2 * axis + side, t))
            one = halo_copy(phase, i, send, recv)
            one.start()
            copies.append(one)
        sent.extend(copies)
        return copies

    def halo_recv(axis, copies, recv):
        for one in copies:
            one.wait_recv()
        return [
            [recv[place(2 * axis + 1 - side, b), side] for b in range(4)] for side in range(2)
        ]

    def onehot(name):
        start, rows, cols = PLACES[name]
        return tab[start : start + rows, 0:cols]

    def permuted(name, value):
        return mm(onehot(name), value).astype(BF)

    loads[2].wait()
    for b in range(4):
        rx[5 + b, 0] = feats[b, 448:512, :]
        rx[5 + b, 1] = feats[b, 0:64, :]
    for side in range(2):
        for i, t in enumerate(SHIFTS):
            rows = slice(448, 512) if side == 0 else slice(0, 64)
            sx[i, side] = feats[pick(side, t), rows, :]
    pl.semaphore_wait(barrier, 4 + 1 + N_PLANE - 1 + N_Z - 1)
    copies = [halo_copy(0, i, sx, rx) for i in range(4)]
    for one in copies:
        one.start()
    sent.extend(copies)

    loads[3].wait()

    def x_layer(s, chunk, halo):
        rows = []
        for xq in range(4):
            x = 2 * xq + s - 1
            for b in range(4):
                if x < 0 or x > 7:
                    rows.append(halo[0 if x < 0 else 1][b][16 * chunk : 16 * chunk + 16])
                else:
                    rows.append(feats[b, 64 * x + 16 * chunk : 64 * x + 16 * chunk + 16, :])
        return jnp.concatenate(rows, axis=0)

    def put_rows(ref, y, z, count, lanes, value):
        ref[pl.ds(y * 10 + z, count), :, lanes] = value

    for chunk in range(4):
        both = jnp.concatenate([x_layer(1, chunk, None), x_layer(2, chunk, None)], axis=1)
        out = permuted("swap", both).reshape(2, 8, 16, 256)
        for j in range(2):
            put_rows(bf, 2 * chunk + j + 1, 1, 8, slice(128, 384), out[j])

    halo = halo_recv(0, copies, rx)
    for chunk in range(4):
        both = jnp.concatenate([x_layer(0, chunk, halo), x_layer(3, chunk, halo)], axis=1)
        out = permuted("swap", both).reshape(2, 8, 16, 256)
        for j in range(2):
            put_rows(bf, 2 * chunk + j + 1, 1, 8, slice(0, 128), out[j, :, :, 0:128])
            put_rows(bf, 2 * chunk + j + 1, 1, 8, slice(384, 512), out[j, :, :, 128:256])

    for side in range(2):
        y = 8 if side == 0 else 1
        layer = bf[y * 10 + 1 : y * 10 + 9].reshape(128, 512)
        flat = jnp.concatenate([layer[:, 0:256], layer[:, 256:512]], axis=0)
        faces = permuted("send_y", flat).reshape(4, 48, 256)
        oy[side] = faces
        ry[5:9, side] = faces
    copies = halo_send(1, 1, lambda side, b: oy[side, b], sy, ry)

    for one in loads[4:]:
        one.wait()
    cot_rows = jnp.concatenate(
        [cot[b, 16 * xq : 16 * xq + 16, :] for xq in range(4) for b in range(4)], axis=0
    )
    cot_perm = permuted("swap", cot_rows)
    cotp[...] = cot_perm

    def down_weight(j, k):
        return jnp.concatenate([wd[2 * j + k], wd[4 + 2 * j + k]], axis=0)

    for j in range(2):
        for k in range(2):
            out = mm_nt(cot_perm, down_weight(j, k)).reshape(4, 4, 16, 256)
            for zq in range(4):
                gh[j, 2 * zq + k] = out[:, zq]

    def weights(k9, carry):
        for s in range(4):
            for xl in range(2):
                dx = s - xl
                fwd_at = (pl.ds(s * 128, 128), pl.ds(xl * 128, 128))
                bwd_at = (pl.ds(xl * 128, 128), pl.ds(s * 128, 128))
                if 0 <= dx <= 2:
                    wf[(k9,) + fwd_at] = wc[9 * dx + k9]
                    wb[(k9,) + bwd_at] = wc[9 * (2 - dx) + 8 - k9]
                else:
                    wf[(k9,) + fwd_at] = jnp.zeros((128, 128), BF)
                    wb[(k9,) + bwd_at] = jnp.zeros((128, 128), BF)
        return carry

    lax.fori_loop(0, 9, weights, 0)

    def tall(values, rows):
        pad = jnp.zeros((rows - values[0].shape[0], values[0].shape[1]), BF)
        return jnp.concatenate([v for value in values for v in (value, pad)], axis=0)

    halo = halo_recv(1, copies, ry)
    for side in range(2):
        y = 0 if side == 0 else 9
        out = permuted("recv_y", tall(halo[side], 64))
        put_rows(bf, y, 1, 8, slice(0, 256), out[0:128].reshape(8, 16, 256))
        put_rows(bf, y, 1, 8, slice(256, 512), out[128:256].reshape(8, 16, 256))

    for side in range(2):
        z = 8 if side == 0 else 1
        near = [bf[y * 10 + z, :, 0:256] for y in range(10)]
        far = [bf[y * 10 + z, :, 256:512] for y in range(10)]
        flat = jnp.concatenate(near + far + [jnp.zeros((64, 256), BF)], axis=0)
        faces = permuted("send_z", flat).reshape(4, 64, 256)
        oz[side] = faces
        rz[5:9, side] = faces
    copies = halo_send(2, 2, lambda side, b: oz[side, b], sz, rz)
    bg[100:112] = jnp.zeros((12, 16, 512), BF)
    dwf[2, 1, 5] = jnp.zeros((128, 128), F32)
    def window(ref, y, z, count):
        lower = ref[pl.ds(y * 10 + z, count)]
        upper = ref[pl.ds(y * 10 + 10 + z, count)]
        return jnp.concatenate([lower, upper], axis=0).reshape(32 * count, 512)

    def activate(pre, grad):
        sig = 1.0 / (1.0 + jnp.exp(-pre))
        hidden = (pre * sig).astype(BF).reshape(-1, 16, 256)
        grad = (grad * sig * (1.0 + pre * (1.0 - sig))).astype(BF)
        return hidden, grad.reshape(-1, 16, 256)

    def inner(yq, carry):
        pre = jnp.zeros((192, 256), F32)
        for k9 in range(9):
            pre = pre + mm(window(bf, 2 * yq + k9 // 3, 1 + k9 % 3, 6), wf[k9])
        grad = jnp.concatenate([gh[j, 1:7, yq] for j in range(2)], axis=0).reshape(192, 256)
        hidden, grad = activate(pre, grad)
        for j in range(2):
            hid[j, 1:7, yq] = hidden[6 * j : 6 * j + 6]
            bg[pl.ds((2 * yq + j + 1) * 10 + 2, 6), :, 128:384] = grad[6 * j : 6 * j + 6]
        return carry

    lax.fori_loop(0, 4, inner, 0)

    middle = [(y, z) for y in range(8) for z in range(1, 7)]
    outer = [(y, z) for y in range(8) for z in (0, 7)]
    groups = [middle[0:16], middle[16:32], middle[32:48], outer]

    def tiles(ref, group, dy, dz):
        return jnp.concatenate([ref[(y + dy) * 10 + z + dz] for y, z in group], axis=0)

    def turn(at):
        gpt[at] = tiles(bg, groups[at], 1, 1)[:, 128:384].astype(F32).T.astype(BF)

    def grad_conv(part, chosen, last):
        for dz in range(3):
            first = jnp.zeros((256, 256), F32)
            second = jnp.zeros((256, 256), F32)
            for at in chosen:
                rows = tiles(bf, groups[at], part, dz)
                first = first + mm(gpt[at], rows[:, 0:256])
                second = second + mm(gpt[at], rows[:, 256:512])
            taps = (
                first[0:128, 0:128] + first[128:256, 128:256],
                first[0:128, 128:256] + second[128:256, 0:128],
                second[0:128, 0:128] + second[128:256, 128:256],
            )
            for dx in range(3):
                slot = dx * 3 + dz
                to = (part, slot // 6, slot % 6)
                dwf[to] = (dwf[to] + taps[dx]).T if last else taps[dx]

    for at in range(3):
        turn(at)
    for part in range(3):
        grad_conv(part, (0, 1, 2), False)

    halo = halo_recv(2, copies, rz)
    for side in range(2):
        z = 0 if side == 0 else 9
        out = permuted("recv_z", jnp.concatenate(halo[side], axis=0))
        for y in range(10):
            bf[y * 10 + z, :, 0:256] = out[16 * y : 16 * y + 16]
            bf[y * 10 + z, :, 256:512] = out[160 + 16 * y : 160 + 16 * y + 16]

    pre = jnp.zeros((256, 256), F32)
    for k9 in range(9):
        pre = pre + mm(tiles(bf, outer, k9 // 3, k9 % 3), wf[k9])
    grad = jnp.concatenate([gh[y % 2, z, y // 2] for y, z in outer], axis=0)
    hidden, grad = activate(pre, grad)
    for at, (y, z) in enumerate(outer):
        hid[y % 2, z, y // 2] = hidden[at]
        bg[(y + 1) * 10 + z + 1, :, 128:384] = grad[at]

    for side in range(2):
        z = 8 if side == 0 else 1
        flat = jnp.concatenate([bg[y * 10 + z, :, 128:384] for y in range(1, 9)], axis=0)
        faces = permuted("send_gz", flat).reshape(4, 32, 256)
        ogz[side] = faces
        rgz[5:9, side] = faces
    copies = halo_send(3, 2, lambda side, b: ogz[side, b], sgz, rgz)

    def core_copy(part):
        return pltpu.make_async_remote_copy(
            src_ref=s1.at[part], dst_ref=r1.at[part], send_sem=cs.at[part], recv_sem=cr.at[part],
            device_id=in_space(sibling), device_id_type=MESH,
        )

    def core_send(part):
        s1[part] = dwf[part, 1 - core].reshape(768, 128).astype(BF)
        core_copy(part).start()

    def each(count, act):
        def body(k, carry):
            act(k)
            return carry

        lax.fori_loop(1, count, body, 0)

    plane_group, z_group = (N_PLANE, plane, in_plane), (N_Z, zpos, in_z)
    order = [(plane_group, z_group), (plane_group, z_group), (z_group, plane_group)]

    def chunk(part, index):
        size = 48 // order[part][0][0]
        return pl.ds(index * size, size)

    def scatter_copy(part, k):
        count, mine, to = order[part][0]
        return pltpu.make_async_remote_copy(
            src_ref=s2.at[part, chunk(part, lax.rem(mine + k, count))],
            dst_ref=r2.at[part, chunk(part, mine)],
            send_sem=xs.at[part], recv_sem=xr.at[part],
            device_id=to(k), device_id_type=MESH,
        )

    def sum_copy(part, k):
        _, mine, to = order[part][1]
        block = r3.at[part, chunk(part, mine)]
        return pltpu.make_async_remote_copy(
            src_ref=block, dst_ref=block, send_sem=zs.at[part], recv_sem=zr.at[part],
            device_id=to(k), device_id_type=MESH,
        )

    def gather_copy(part, k):
        _, mine, to = order[part][0]
        return pltpu.make_async_remote_copy(
            src_ref=fin.at[part, chunk(part, 0)], dst_ref=sums_o.at[part, core, chunk(part, mine)],
            send_sem=as_.at[part], recv_sem=ar.at[part],
            device_id=to(k), device_id_type=MESH,
        )

    def hand_copy(part):
        half = sums_o.at[part, core]
        return pltpu.make_async_remote_copy(
            src_ref=half, dst_ref=half, send_sem=fs.at[part], recv_sem=fr.at[part],
            device_id=in_space(sibling), device_id_type=MESH,
        )

    def all_bytes(ref, sem):
        pltpu.make_async_copy(ref, ref, sem).wait()

    def sent_bytes(part, stage):
        size = 48 // order[part][0][0]
        return pl.ds(0, size * (order[part][stage][0] - 1))

    def added(ref, part, count):
        total = ref[part, chunk(part, 0)].astype(F32)
        for i in range(1, count):
            total = total + ref[part, chunk(part, i)].astype(F32)
        return total.astype(BF)

    def scatter_send(part):
        core_copy(part).wait_recv()
        mine = dwf[part, core].reshape(768, 128) + r1[part].astype(F32)
        s2[part] = mine.astype(BF).reshape(48, 16, 128)
        count, index, _ = order[part][0]
        each(count, lambda k: scatter_copy(part, k).start())
        r2[part, chunk(part, index)] = s2[part, chunk(part, index)]

    def sum_send(part):
        all_bytes(r2.at[part, sent_bytes(part, 0)], xr.at[part])
        count, index, _ = order[part][1]
        r3[part, chunk(part, index)] = added(r2, part, order[part][0][0])
        each(count, lambda k: sum_copy(part, k).start())

    def gather_send(part):
        all_bytes(r3.at[part, sent_bytes(part, 1)], zr.at[part])
        count, index, _ = order[part][0]
        total = added(r3, part, order[part][1][0])
        fin[part, chunk(part, 0)] = total
        each(count, lambda k: gather_copy(part, k).start())
        sums_o[part, core, chunk(part, index)] = total

    def hand_over(part):
        all_bytes(sums_o.at[part, core, sent_bytes(part, 0)], ar.at[part])
        hand_copy(part).start()

    def finish(part):
        hand_copy(part).wait_recv()
        core_copy(part).wait_send()
        all_bytes(s2.at[part, sent_bytes(part, 0)], xs.at[part])
        all_bytes(r3.at[part, sent_bytes(part, 1)], zs.at[part])
        all_bytes(sums_o.at[part, core, sent_bytes(part, 0)], as_.at[part])
        hand_copy(part).wait_send()

    def down_rows(j, k):
        tiles = [hid[j, 2 * zq + k, yq] for yq in range(4) for zq in range(4)]
        return jnp.concatenate(tiles, axis=0)

    cot_t = cotp[...].astype(F32).T.astype(BF)
    for j in range(2):
        for k in range(2):
            out = mm(cot_t, down_rows(j, k))
            for i in range(2):
                tap = 4 * i + 2 * j + k
                dwf[tap // 3, 1, 3 + tap % 3] = out[:, 128 * i : 128 * i + 128].T
    turn(3)
    for part in range(3):
        grad_conv(part, (3,), True)
        core_send(part)
    for part in range(3):
        scatter_send(part)

    halo = halo_recv(2, copies, rgz)
    for side in range(2):
        z = 0 if side == 0 else 9
        out = permuted("recv_gz", jnp.concatenate(halo[side], axis=0))
        for y in range(8):
            bg[(y + 1) * 10 + z, :, 128:384] = out[16 * y : 16 * y + 16]

    for side in range(2):
        y = 8 if side == 0 else 1
        flat = bg[y * 10 : y * 10 + 10, :, 128:384].reshape(160, 256)
        flat = jnp.concatenate([flat, jnp.zeros((96, 256), BF)], axis=0)
        faces = permuted("send_gy", flat).reshape(4, 48, 256)
        ogy[side] = faces
        rgy[5:9, side] = faces
    copies = halo_send(4, 1, lambda side, b: ogy[side, b], sgy, rgy)
    total = jnp.zeros((256, 128), F32)
    for j in range(2):
        for k in range(2):
            total = total + mm(down_rows(j, k), down_weight(j, k))
    out = permuted("swap", total.astype(BF))
    for b in range(4):
        for xq in range(4):
            at = 16 * (4 * xq + b)
            pooled_o[b, 16 * xq : 16 * xq + 16, :] = out[at : at + 16]
    for part in range(3):
        sum_send(part)
    halo = halo_recv(1, copies, rgy)
    for side in range(2):
        y = 0 if side == 0 else 9
        out = permuted("recv_gy", tall(halo[side], 64))
        put_rows(bg, y, 0, 10, slice(128, 384), out.reshape(10, 16, 256))

    for group in range(7):
        inside = bg[16 * group : 16 * group + 16, :, 128:384].reshape(256, 256)
        out = permuted("send_gx", inside)
        for b in range(4):
            rows = slice(16 * group, 16 * group + 16)
            for side in range(2):
                lanes = slice(128, 256) if side == 0 else slice(0, 128)
                face = out[64 * side + 16 * b : 64 * side + 16 * b + 16, lanes]
                ogx[side, b, rows] = face
                rgx[5 + b, side, rows] = face
    copies = halo_send(5, 0, lambda side, b: ogx[side, b], sgx, rgx)
    for group in range(7):
        at = slice(16 * group, 16 * group + 16)
        inside = bg[at, :, 128:384].reshape(256, 256)
        bg[at, :, 0:128] = permuted("low", inside[:, 128:256]).reshape(16, 16, 128)
        bg[at, :, 384:512] = permuted("high", inside[:, 0:128]).reshape(16, 16, 128)
    gather_send(0)
    gather_send(1)
    halo = halo_recv(0, copies, rgx)
    for group in range(7):
        at = slice(16 * group, 16 * group + 16)
        rows = jnp.concatenate([halo[side][b][at] for side in range(2) for b in range(4)], axis=0)
        out = permuted("insert", rows)
        bg[at, :, 0:128] = bg[at, :, 0:128] + out[0:256].reshape(16, 16, 128)
        bg[at, :, 384:512] = bg[at, :, 384:512] + out[256:512].reshape(16, 16, 128)

    def backward(yq, carry):
        grad = jnp.zeros((256, 256), F32)
        for k9 in range(9):
            grad = grad + mm_nt(window(bg, 2 * yq + k9 // 3, k9 % 3, 8), wb[k9])
        out = permuted("swap", grad.astype(BF))
        for xq in range(4):
            for b in range(4):
                tile = out[16 * (4 * xq + b) : 16 * (4 * xq + b) + 16]
                for xl in range(2):
                    at = pl.ds(pl.multiple_of(64 * (2 * xq + xl) + 16 * yq, 16), 16)
                    dfeats_o[b, at, :] = tile[:, 128 * xl : 128 * xl + 128]
        return carry

    gather_send(2)
    lax.fori_loop(0, 4, backward, 0)
    for part in range(3):
        hand_over(part)
    for one in sent:
        one.wait_send()
    for part in range(3):
        finish(part)


def epilogue(norm, sums, pooled, dfeats, pooled_o, dfeats_o, conv_o, down_o, conv, down, sem):
    copies = [
        pltpu.make_async_copy(dfeats, dfeats_o, sem.at[0]),
        pltpu.make_async_copy(pooled, pooled_o, sem.at[1]),
    ]
    copies[0].start()
    copies[1].start()
    for part in range(3):
        conv[part] = (sums[part, 0:9].astype(F32) * norm).reshape(3, 3, 128, 128)
        one = pltpu.make_async_copy(conv.at[part], conv_o.at[:, part], sem.at[2 + part])
        one.start()
        copies.append(one)
    for tap in range(8):
        down[tap] = sums[tap // 3, 9 + tap % 3].astype(F32) * norm
    one = pltpu.make_async_copy(down, down_o, sem.at[5])
    one.start()
    copies.append(one)
    for one in copies:
        one.wait()


def per_device(feats, w_conv, w_down, cotangent, nbr_owner, nbr_slot):
    def buf(*shape, dtype=BF):
        return pltpu.VMEM(shape, dtype)

    def halo(rows, lanes, own=True):
        bufs = [buf(4, 2, rows, lanes), buf(9, 2, rows, lanes)]
        return ([buf(2, 4, rows, lanes)] if own else []) + bufs

    def in_hbm(value):
        return pltpu.with_memory_space_constraint(value, pltpu.HBM)

    vmem = pl.BlockSpec(memory_space=pltpu.VMEM)
    hbm = pl.BlockSpec(memory_space=pltpu.HBM)
    dma = pltpu.SemaphoreType.DMA
    operands = (
        feats[0], w_conv, w_down, cotangent[0], jnp.asarray(TABLES, BF), nbr_owner, nbr_slot
    )
    pooled, d_feats, sums = pl.pallas_call(
        kernel,
        out_shape=(
            pltpu.VMEM((4, 64, 128), BF),
            pltpu.VMEM((4, 512, 128), BF),
            pltpu.VMEM((3, 2, 48, 16, 128), BF),
        ),
        in_specs=[hbm] * 7,
        out_specs=(vmem, vmem, vmem),
        scratch_shapes=[
            buf(4, 512, 128), buf(27, 128, 128), buf(8, 128, 128), buf(4, 64, 128),
            buf(*TABLES.shape),
            pltpu.SMEM((1, 4, 6), jnp.int32), pltpu.SMEM((1, 4, 6), jnp.int32),
            buf(100, 16, 512), buf(112, 16, 512),
            buf(9, 512, 256), buf(9, 256, 512),
            buf(2, 8, 4, 16, 256, dtype=F32), buf(2, 8, 4, 16, 256),
            buf(4, 256, 256), buf(256, 128),
            buf(3, 2, 6, 128, 128, dtype=F32),
            *halo(64, 128, own=False), *halo(48, 256), *halo(64, 256),
            *halo(32, 256), *halo(48, 256), *halo(112, 128),
            buf(3, 768, 128), buf(3, 768, 128),
            buf(3, 48, 16, 128), buf(3, 48, 16, 128), buf(3, 96, 16, 128), buf(3, 6, 16, 128),
            dma((7,)),
            dma((6, 4)), dma((6, 4)),
            *([dma((3,))] * 10),
        ],
        compiler_params=pltpu.CompilerParams(
            collective_id=0, has_side_effects=True, vmem_limit_bytes=48 * 1024 * 1024
        ),
    )(*[in_hbm(one) for one in operands])
    norm = 1.0 / float(lax.axis_size("rep") * lax.axis_size("space") * 4 * 512) ** 0.5
    pooled, d_feats, conv, down = pl.pallas_call(
        functools.partial(epilogue, norm),
        out_shape=(
            jax.ShapeDtypeStruct((4, 64, 128), BF),
            jax.ShapeDtypeStruct((4, 512, 128), BF),
            jax.ShapeDtypeStruct((3, 3, 3, 128, 128), F32),
            jax.ShapeDtypeStruct((8, 128, 128), F32),
        ),
        in_specs=[vmem] * 3,
        out_specs=[hbm] * 4,
        scratch_shapes=[buf(3, 3, 3, 128, 128, dtype=F32), buf(8, 128, 128, dtype=F32), dma((6,))],
        compiler_params=pltpu.CompilerParams(vmem_limit_bytes=24 * 1024 * 1024),
    )(sums.reshape(3, 12, 128, 128), pooled, d_feats)
    return (pooled[None], d_feats[None], conv.reshape(27, 128, 128), down)


def solution(mesh):
    placed = (
        P("rep", "space", None, None),
        P(),
        P(),
        P("rep", "space", None, None),
        P("rep", "space", None),
        P("rep", "space", None),
    )
    return jax.shard_map(
        per_device,
        mesh=mesh,
        in_specs=placed,
        out_specs=(P("rep", "space", None, None), P("rep", "space", None, None), P(), P()),
        check_vma=False,
    )
```

```python
import functools

import jax
import jax.numpy as jnp
import numpy as np
from jax import lax
from jax.experimental import pallas as pl
from jax.experimental.pallas import tpu as pltpu
from jax.sharding import PartitionSpec as P

BF = jnp.bfloat16
F32 = jnp.float32
MESH = pl.DeviceIdType.MESH
SHIFTS = (-2, -1, 1, 2)
N_SPACE = 64
N_PLANE = 16
N_Z = 8


def onehot_tables():
    tables = {}

    def table(name, rows, cols):
        tables[name] = np.zeros((rows, cols), np.float32)
        return tables[name]

    swap = table("swap", 256, 256)
    for p in range(16):
        for q in range(16):
            swap[p * 16 + q, q * 16 + p] = 1
    send_y, recv_y = table("send_y", 64, 256), table("recv_y", 256, 384)
    send_z, recv_z = table("send_z", 192, 384), table("recv_z", 384, 512)
    move, back = table("move", 128, 128), table("back", 128, 128)
    send_gy, recv_gy = table("send_gy", 192, 256), table("recv_gy", 160, 256)
    send_gx = table("send_gx", 128, 256)
    low, high = table("low", 256, 256), table("high", 256, 256)
    insert = table("insert", 512, 128)
    for b in range(4):
        for xq in range(4):
            row = xq * 4 + b
            for z in range(8):
                at = z * 16 + row
                recv_y[at, 128 + at - 4 if xq > 0 else 256 + b * 16 + z] = 1
                recv_y[128 + at, at + 4 if xq < 3 else 264 + b * 16 + z] = 1
                if xq == 0:
                    send_y[b * 16 + z, at] = 1
                if xq == 3:
                    send_y[b * 16 + 8 + z, 128 + at] = 1
                move[b * 32 + z * 4 + xq, at] = 1
                back[at, b * 32 + z * 4 + xq] = 1
            for y in range(10):
                at = y * 16 + row

                def near(s, column):
                    if 1 <= y <= 8:
                        return (s - 1) * 128 + (y - 1) * 16 + column * 4 + b
                    return 276 + b * 48 + ((y > 0) * 2 + s - 1) * 4 + column

                recv_z[at, near(2, xq - 1) if xq > 0 else 256 + b * 48 + y] = 1
                recv_z[160 + at, near(1, xq + 1) if xq < 3 else 266 + b * 48 + y] = 1
                if xq == 0:
                    send_z[b * 48 + y, at] = 1
                if xq == 3:
                    send_z[b * 48 + 10 + y, 160 + at] = 1
                if y in (0, 9):
                    for s in (1, 2):
                        edge = 288 + 32 * s + (y > 0) * 16 + row
                        recv_z[edge, near(s, xq)] = 1
                        send_z[b * 48 + 20 + ((y > 0) * 2 + s - 1) * 4 + xq, edge] = 1
                send_gy[b * 48 + y * 4 + xq, y * 16 + row] = 1
                recv_gy[y * 16 + row, b * 64 + y * 4 + xq] = 1
            for k in range(16):
                if xq >= 1:
                    low[k * 16 + row, k * 16 + row - 4] = 1
                if xq <= 2:
                    high[k * 16 + row, k * 16 + row + 4] = 1
        for k in range(16):
            send_gx[b * 16 + k, k * 16 + 12 + b] = 1
            send_gx[64 + b * 16 + k, k * 16 + b] = 1
            insert[k * 16 + b, b * 16 + k] = 1
            insert[256 + k * 16 + 12 + b, 64 + b * 16 + k] = 1
    places, parts, start = {}, [], 0
    for name, value in tables.items():
        rows, cols = value.shape
        places[name] = (start, rows, cols)
        parts.append(np.pad(value, ((0, 0), (0, 512 - cols))))
        start += rows
    return places, np.concatenate(parts)


PLACES, TABLES = onehot_tables()


def mm(left, right):
    return jnp.dot(left, right, preferred_element_type=F32)


def mm_nt(left, right):
    return lax.dot_general(left, right, (((1,), (1,)), ((), ())), preferred_element_type=F32)


def kernel(
    feats_h, wc_h, wd_h, cot_h, tab_h, own_h, slot_h,
    pooled_o, dfeats_o, sums_o,
    feats, wc, wd, cot, tab, own_s, slot_s, bf, bg, wf, wb, gh, hid, gpt, cotp, dwf,
    sx, rx, oy, sy, ry, oz, sz, rz, oyi, syi, ryi, ozi, szi, rzi, ogz, sgz, rgz, ogy, sgy, rgy, ogx, sgx, rgx,
    s1, r1, s2, r2, r3, fin,
    lsem, hs, hr, cs, cr, xs, xr, zs, zr, as_, ar, fs, fr,
):
    pos = lax.axis_index("space")
    rep = lax.axis_index("rep")
    core = lax.rem(pos, 2)
    zpos = lax.rem(lax.div(pos, 2), 8)
    xpos = lax.div(pos, 16)
    plane = xpos * 4 + rep
    sibling = pos + 1 - 2 * core

    def in_space(to):
        return {"space": to, "rep": rep}

    def in_plane(k):
        to = lax.rem(plane + k, N_PLANE)
        return {"space": lax.div(to, 4) * 16 + lax.rem(pos, 16), "rep": lax.rem(to, 4)}

    def in_z(k):
        to = lax.rem(zpos + k, N_Z)
        return {"space": xpos * 16 + to * 2 + core, "rep": rep}

    loads = [
        pltpu.make_async_copy(src, dst, lsem.at[i])
        for i, (src, dst) in enumerate(
            (
                (own_h, own_s), (slot_h, slot_s), (feats_h, feats), (tab_h, tab),
                (cot_h, cot), (wc_h, wc), (wd_h, wd),
            )
        )
    ]
    for one in loads:
        one.start()

    barrier = pltpu.get_barrier_semaphore()
    for t in SHIFTS:
        to = lax.rem(pos + t + N_SPACE, N_SPACE)
        pl.semaphore_signal(barrier, inc=1, device_id=in_space(to), device_id_type=MESH)
    pl.semaphore_signal(barrier, inc=1, device_id=in_space(sibling), device_id_type=MESH)

    def greet_plane(k, carry):
        pl.semaphore_signal(barrier, inc=1, device_id=in_plane(k), device_id_type=MESH)
        return carry

    def greet_z(k, carry):
        pl.semaphore_signal(barrier, inc=1, device_id=in_z(k), device_id_type=MESH)
        return carry

    lax.fori_loop(1, N_PLANE, greet_plane, 0)
    lax.fori_loop(1, N_Z, greet_z, 0)

    loads[0].wait()
    loads[1].wait()

    owners = [[own_s[0, b, d] for d in range(6)] for b in range(4)]
    slots = [[slot_s[0, b, d] for d in range(6)] for b in range(4)]

    def pick(d, t):
        found = jnp.int32(0)
        for b in range(1, 4):
            hit = (owners[b][d] == pos + t) & (owners[b][d] >= 0)
            found = jnp.where(hit, b, found)
        return found

    def place(d, b):
        gap = pos - owners[b][d]
        far = jnp.clip(jnp.where(gap < 0, gap + 2, gap + 1), 0, 3)
        near = jnp.clip(5 + slots[b][d], 5, 8)
        return jnp.where(owners[b][d] < 0, 4, jnp.where(gap == 0, near, far))

    for ref in (rx, ry, rz, ryi, rzi, rgz, rgy, rgx):
        ref[4] = jnp.zeros(ref.shape[1:], BF)

    def halo_copy(phase, i, send, recv):
        to = lax.rem(pos + SHIFTS[i] + N_SPACE, N_SPACE)
        return pltpu.make_async_remote_copy(
            src_ref=send.at[i],
            dst_ref=recv.at[i],
            send_sem=hs.at[phase, i],
            recv_sem=hr.at[phase, i],
            device_id=in_space(to),
            device_id_type=MESH,
        )

    sent = []

    def halo_send(phase, axis, own, send, recv):
        copies = []
        for i, t in enumerate(SHIFTS):
            for side in range(2):
                send[i, side] = own(side, pick(2 * axis + side, t))
            one = halo_copy(phase, i, send, recv)
            one.start()
            copies.append(one)
        sent.extend(copies)
        return copies

    def halo_recv(axis, copies, recv):
        for one in copies:
            one.wait_recv()
        return [
            [recv[place(2 * axis + 1 - side, b), side] for b in range(4)] for side in range(2)
        ]

    def onehot(name):
        start, rows, cols = PLACES[name]
        return tab[start : start + rows, 0:cols]

    def permuted(name, value):
        return mm(onehot(name), value).astype(BF)

    loads[2].wait()
    for b in range(4):
        rx[5 + b, 0] = feats[b, 448:512, :]
        rx[5 + b, 1] = feats[b, 0:64, :]
    for side in range(2):
        for i, t in enumerate(SHIFTS):
            rows = slice(448, 512) if side == 0 else slice(0, 64)
            sx[i, side] = feats[pick(side, t), rows, :]
    pl.semaphore_wait(barrier, 4 + 1 + N_PLANE - 1 + N_Z - 1)
    copies = [halo_copy(0, i, sx, rx) for i in range(4)]
    for one in copies:
        one.start()
    sent.extend(copies)

    loads[3].wait()

    def x_layer(s, chunk, halo):
        rows = []
        for xq in range(4):
            x = 2 * xq + s - 1
            for b in range(4):
                if x < 0 or x > 7:
                    rows.append(halo[0 if x < 0 else 1][b][16 * chunk : 16 * chunk + 16])
                else:
                    rows.append(feats[b, 64 * x + 16 * chunk : 64 * x + 16 * chunk + 16, :])
        return jnp.concatenate(rows, axis=0)

    def put_rows(ref, y, z, count, lanes, value):
        ref[pl.ds(y * 10 + z, count), :, lanes] = value

    for chunk in range(4):
        both = jnp.concatenate([x_layer(1, chunk, None), x_layer(2, chunk, None)], axis=1)
        out = permuted("swap", both).reshape(2, 8, 16, 256)
        for j in range(2):
            put_rows(bf, 2 * chunk + j + 1, 1, 8, slice(128, 384), out[j])

    def inner_faces(at, own, recv):
        for side in range(2):
            flat = jnp.concatenate([bf[i, :, 128:384] for i in at(side)], axis=0)
            faces = permuted("move", flat).reshape(4, 32, 256)
            own[side] = faces
            recv[5:9, side] = faces

    inner_faces(lambda side: [(8 - 7 * side) * 10 + z for z in range(1, 9)], oyi, ryi)
    copies_y = halo_send(6, 1, lambda side, b: oyi[side, b], syi, ryi)
    inner_faces(lambda side: [y * 10 + 8 - 7 * side for y in range(1, 9)], ozi, rzi)
    copies_z = halo_send(7, 2, lambda side, b: ozi[side, b], szi, rzi)

    halo = halo_recv(0, copies, rx)
    for chunk in range(4):
        both = jnp.concatenate([x_layer(0, chunk, halo), x_layer(3, chunk, halo)], axis=1)
        out = permuted("swap", both).reshape(2, 8, 16, 256)
        for j in range(2):
            put_rows(bf, 2 * chunk + j + 1, 1, 8, slice(0, 128), out[j, :, :, 0:128])
            put_rows(bf, 2 * chunk + j + 1, 1, 8, slice(384, 512), out[j, :, :, 128:256])

    def both_sides(make):
        return jnp.concatenate([make(0), make(1)], axis=1)

    def y_rows(side):
        at = (8 - 7 * side) * 10
        low, high = bf[at + 1 : at + 9, :, 0:128], bf[at + 1 : at + 9, :, 384:512]
        return jnp.concatenate([low.reshape(128, 128), high.reshape(128, 128)], axis=0)

    def rim_faces(name, rows, count, own, recv):
        out = permuted(name, both_sides(rows)).reshape(4, count, 256)
        for side in range(2):
            own[side] = out[:, :, 128 * side : 128 * side + 128]
            recv[5:9, side] = out[:, :, 128 * side : 128 * side + 128]

    rim_faces("send_y", y_rows, 16, oy, ry)
    copies = halo_send(1, 1, lambda side, b: oy[side, b], sy, ry)

    for one in loads[4:]:
        one.wait()
    cot_rows = jnp.concatenate(
        [cot[b, 16 * xq : 16 * xq + 16, :] for xq in range(4) for b in range(4)], axis=0
    )
    cot_perm = permuted("swap", cot_rows)
    cotp[...] = cot_perm

    def down_weight(j, k):
        return jnp.concatenate([wd[2 * j + k], wd[4 + 2 * j + k]], axis=0)

    for j in range(2):
        for k in range(2):
            out = mm_nt(cot_perm, down_weight(j, k)).reshape(4, 4, 16, 256)
            for zq in range(4):
                gh[j, 2 * zq + k] = out[:, zq]

    def weights(k9, carry):
        for s in range(4):
            for xl in range(2):
                dx = s - xl
                fwd_at = (pl.ds(s * 128, 128), pl.ds(xl * 128, 128))
                bwd_at = (pl.ds(xl * 128, 128), pl.ds(s * 128, 128))
                if 0 <= dx <= 2:
                    wf[(k9,) + fwd_at] = wc[9 * dx + k9]
                    wb[(k9,) + bwd_at] = wc[9 * (2 - dx) + 8 - k9]
                else:
                    wf[(k9,) + fwd_at] = jnp.zeros((128, 128), BF)
                    wb[(k9,) + bwd_at] = jnp.zeros((128, 128), BF)
        return carry

    lax.fori_loop(0, 9, weights, 0)

    def tall(values, rows):
        pad = jnp.zeros((rows - values[0].shape[0], values[0].shape[1]), BF)
        return jnp.concatenate([v for value in values for v in (value, pad)], axis=0)

    def inner_halo(axis, copies, recv):
        halo = halo_recv(axis, copies, recv)
        return [permuted("back", jnp.concatenate(halo[side], axis=0)) for side in range(2)]

    def rim_rows(inside, halo, rows):
        def one(side):
            pad = jnp.zeros((rows - 256 - 4 * halo[side][0].shape[0], 128), BF)
            parts = [inside[side][:, 0:128], inside[side][:, 128:256], *halo[side], pad]
            return jnp.concatenate(parts, axis=0)

        return both_sides(one)

    inside = inner_halo(1, copies_y, ryi)
    for side in range(2):
        put_rows(bf, 9 * side, 1, 8, slice(128, 384), inside[side].reshape(8, 16, 256))
    halo = halo_recv(1, copies, ry)
    out = permuted("recv_y", rim_rows(inside, halo, 384)).reshape(2, 8, 16, 256)
    for side in range(2):
        lanes = slice(128 * side, 128 * side + 128)
        put_rows(bf, 9 * side, 1, 8, slice(0, 128), out[0, :, :, lanes])
        put_rows(bf, 9 * side, 1, 8, slice(384, 512), out[1, :, :, lanes])

    def z_rows(side):
        at = 8 - 7 * side
        parts = [bf[y * 10 + at, :, 0:128] for y in range(10)]
        parts += [bf[y * 10 + at, :, 384:512] for y in range(10)]
        parts += [bf[y * 10 + at, :, 128 * s : 128 * s + 128] for s in (1, 2) for y in (0, 9)]
        return jnp.concatenate(parts, axis=0)

    rim_faces("send_z", z_rows, 48, oz, rz)
    copies = halo_send(2, 2, lambda side, b: oz[side, b], sz, rz)
    inside = inner_halo(2, copies_z, rzi)
    for side in range(2):
        for y in range(1, 9):
            bf[y * 10 + 9 * side, :, 128:384] = inside[side][16 * y - 16 : 16 * y]
    bg[100:112] = jnp.zeros((12, 16, 512), BF)
    dwf[2, 1, 5] = jnp.zeros((128, 128), F32)
    def window(ref, y, z, count):
        lower = ref[pl.ds(y * 10 + z, count)]
        upper = ref[pl.ds(y * 10 + 10 + z, count)]
        return jnp.concatenate([lower, upper], axis=0).reshape(32 * count, 512)

    def activate(pre, grad):
        sig = 1.0 / (1.0 + jnp.exp(-pre))
        hidden = (pre * sig).astype(BF).reshape(-1, 16, 256)
        grad = (grad * sig * (1.0 + pre * (1.0 - sig))).astype(BF)
        return hidden, grad.reshape(-1, 16, 256)

    def inner(yq, carry):
        pre = jnp.zeros((192, 256), F32)
        for k9 in range(9):
            pre = pre + mm(window(bf, 2 * yq + k9 // 3, 1 + k9 % 3, 6), wf[k9])
        grad = jnp.concatenate([gh[j, 1:7, yq] for j in range(2)], axis=0).reshape(192, 256)
        hidden, grad = activate(pre, grad)
        for j in range(2):
            hid[j, 1:7, yq] = hidden[6 * j : 6 * j + 6]
            bg[pl.ds((2 * yq + j + 1) * 10 + 2, 6), :, 128:384] = grad[6 * j : 6 * j + 6]
        return carry

    lax.fori_loop(0, 4, inner, 0)

    middle = [(y, z) for y in range(8) for z in range(1, 7)]
    outer = [(y, z) for y in range(8) for z in (0, 7)]
    groups = [middle[0:16], middle[16:32], middle[32:48], outer]

    def tiles(ref, group, dy, dz):
        return jnp.concatenate([ref[(y + dy) * 10 + z + dz] for y, z in group], axis=0)

    def turn(at):
        gpt[at] = tiles(bg, groups[at], 1, 1)[:, 128:384].astype(F32).T.astype(BF)

    def grad_conv(part, chosen, last):
        for dz in range(3):
            first = jnp.zeros((256, 256), F32)
            second = jnp.zeros((256, 256), F32)
            for at in chosen:
                rows = tiles(bf, groups[at], part, dz)
                first = first + mm(gpt[at], rows[:, 0:256])
                second = second + mm(gpt[at], rows[:, 256:512])
            taps = (
                first[0:128, 0:128] + first[128:256, 128:256],
                first[0:128, 128:256] + second[128:256, 0:128],
                second[0:128, 0:128] + second[128:256, 128:256],
            )
            for dx in range(3):
                slot = dx * 3 + dz
                to = (part, slot // 6, slot % 6)
                dwf[to] = (dwf[to] + taps[dx]).T if last else taps[dx]

    for at in range(3):
        turn(at)
    for part in range(3):
        grad_conv(part, (0, 1, 2), False)

    halo = halo_recv(2, copies, rz)
    out = permuted("recv_z", rim_rows(inside, halo, 512)).reshape(24, 16, 256)
    for side in range(2):
        lanes = slice(128 * side, 128 * side + 128)
        for y in range(10):
            bf[y * 10 + 9 * side, :, 0:128] = out[y, :, lanes]
            bf[y * 10 + 9 * side, :, 384:512] = out[10 + y, :, lanes]
        for i, y in enumerate((0, 9)):
            bf[y * 10 + 9 * side, :, 128:256] = out[20 + i, :, lanes]
            bf[y * 10 + 9 * side, :, 256:384] = out[22 + i, :, lanes]

    pre = jnp.zeros((256, 256), F32)
    for k9 in range(9):
        pre = pre + mm(tiles(bf, outer, k9 // 3, k9 % 3), wf[k9])
    grad = jnp.concatenate([gh[y % 2, z, y // 2] for y, z in outer], axis=0)
    hidden, grad = activate(pre, grad)
    for at, (y, z) in enumerate(outer):
        hid[y % 2, z, y // 2] = hidden[at]
        bg[(y + 1) * 10 + z + 1, :, 128:384] = grad[at]

    for side in range(2):
        z = 8 if side == 0 else 1
        flat = jnp.concatenate([bg[y * 10 + z, :, 128:384] for y in range(1, 9)], axis=0)
        faces = permuted("move", flat).reshape(4, 32, 256)
        ogz[side] = faces
        rgz[5:9, side] = faces
    copies = halo_send(3, 2, lambda side, b: ogz[side, b], sgz, rgz)

    def core_copy(part):
        return pltpu.make_async_remote_copy(
            src_ref=s1.at[part], dst_ref=r1.at[part], send_sem=cs.at[part], recv_sem=cr.at[part],
            device_id=in_space(sibling), device_id_type=MESH,
        )

    def core_send(part):
        s1[part] = dwf[part, 1 - core].reshape(768, 128).astype(BF)
        core_copy(part).start()

    def each(count, act):
        def body(k, carry):
            act(k)
            return carry

        lax.fori_loop(1, count, body, 0)

    plane_group, z_group = (N_PLANE, plane, in_plane), (N_Z, zpos, in_z)
    order = [(plane_group, z_group)] * 3

    def chunk(part, index):
        size = 48 // order[part][0][0]
        return pl.ds(index * size, size)

    def scatter_copy(part, k):
        count, mine, to = order[part][0]
        return pltpu.make_async_remote_copy(
            src_ref=s2.at[part, chunk(part, lax.rem(mine + k, count))],
            dst_ref=r2.at[part, chunk(part, mine)],
            send_sem=xs.at[part], recv_sem=xr.at[part],
            device_id=to(k), device_id_type=MESH,
        )

    def sum_copy(part, k):
        _, mine, to = order[part][1]
        block = r3.at[part, chunk(part, mine)]
        return pltpu.make_async_remote_copy(
            src_ref=block, dst_ref=block, send_sem=zs.at[part], recv_sem=zr.at[part],
            device_id=to(k), device_id_type=MESH,
        )

    def gather_copy(part, k):
        _, mine, to = order[part][0]
        return pltpu.make_async_remote_copy(
            src_ref=fin.at[part, chunk(part, 0)], dst_ref=sums_o.at[part, core, chunk(part, mine)],
            send_sem=as_.at[part], recv_sem=ar.at[part],
            device_id=to(k), device_id_type=MESH,
        )

    def hand_copy(part):
        half = sums_o.at[part, core]
        return pltpu.make_async_remote_copy(
            src_ref=half, dst_ref=half, send_sem=fs.at[part], recv_sem=fr.at[part],
            device_id=in_space(sibling), device_id_type=MESH,
        )

    def all_bytes(ref, sem):
        pltpu.make_async_copy(ref, ref, sem).wait()

    def sent_bytes(part, stage):
        size = 48 // order[part][0][0]
        return pl.ds(0, size * (order[part][stage][0] - 1))

    def added(ref, part, count):
        total = ref[part, chunk(part, 0)].astype(F32)
        for i in range(1, count):
            total = total + ref[part, chunk(part, i)].astype(F32)
        return total.astype(BF)

    def scatter_send(part):
        core_copy(part).wait_recv()
        mine = dwf[part, core].reshape(768, 128) + r1[part].astype(F32)
        s2[part] = mine.astype(BF).reshape(48, 16, 128)
        count, index, _ = order[part][0]
        each(count, lambda k: scatter_copy(part, k).start())
        r2[part, chunk(part, index)] = s2[part, chunk(part, index)]

    def sum_send(part):
        all_bytes(r2.at[part, sent_bytes(part, 0)], xr.at[part])
        count, index, _ = order[part][1]
        r3[part, chunk(part, index)] = added(r2, part, order[part][0][0])
        each(count, lambda k: sum_copy(part, k).start())

    def gather_send(part):
        all_bytes(r3.at[part, sent_bytes(part, 1)], zr.at[part])
        count, index, _ = order[part][0]
        total = added(r3, part, order[part][1][0])
        fin[part, chunk(part, 0)] = total
        each(count, lambda k: gather_copy(part, k).start())
        sums_o[part, core, chunk(part, index)] = total

    def hand_over(part):
        all_bytes(sums_o.at[part, core, sent_bytes(part, 0)], ar.at[part])
        hand_copy(part).start()

    def finish(part):
        hand_copy(part).wait_recv()
        core_copy(part).wait_send()
        all_bytes(s2.at[part, sent_bytes(part, 0)], xs.at[part])
        all_bytes(r3.at[part, sent_bytes(part, 1)], zs.at[part])
        all_bytes(sums_o.at[part, core, sent_bytes(part, 0)], as_.at[part])
        hand_copy(part).wait_send()

    def down_rows(j, k):
        tiles = [hid[j, 2 * zq + k, yq] for yq in range(4) for zq in range(4)]
        return jnp.concatenate(tiles, axis=0)

    cot_t = cotp[...].astype(F32).T.astype(BF)
    for j in range(2):
        for k in range(2):
            out = mm(cot_t, down_rows(j, k))
            for i in range(2):
                tap = 4 * i + 2 * j + k
                dwf[tap // 3, 1, 3 + tap % 3] = out[:, 128 * i : 128 * i + 128].T
    turn(3)
    for part in range(3):
        grad_conv(part, (3,), True)
        core_send(part)
    for part in range(3):
        scatter_send(part)

    halo = halo_recv(2, copies, rgz)
    for side in range(2):
        z = 0 if side == 0 else 9
        out = permuted("back", jnp.concatenate(halo[side], axis=0))
        for y in range(8):
            bg[(y + 1) * 10 + z, :, 128:384] = out[16 * y : 16 * y + 16]

    for side in range(2):
        y = 8 if side == 0 else 1
        flat = bg[y * 10 : y * 10 + 10, :, 128:384].reshape(160, 256)
        flat = jnp.concatenate([flat, jnp.zeros((96, 256), BF)], axis=0)
        faces = permuted("send_gy", flat).reshape(4, 48, 256)
        ogy[side] = faces
        rgy[5:9, side] = faces
    copies = halo_send(4, 1, lambda side, b: ogy[side, b], sgy, rgy)
    total = jnp.zeros((256, 128), F32)
    for j in range(2):
        for k in range(2):
            total = total + mm(down_rows(j, k), down_weight(j, k))
    out = permuted("swap", total.astype(BF))
    for b in range(4):
        for xq in range(4):
            at = 16 * (4 * xq + b)
            pooled_o[b, 16 * xq : 16 * xq + 16, :] = out[at : at + 16]
    sum_send(0)
    sum_send(1)
    halo = halo_recv(1, copies, rgy)
    for side in range(2):
        y = 0 if side == 0 else 9
        out = permuted("recv_gy", tall(halo[side], 64))
        put_rows(bg, y, 0, 10, slice(128, 384), out.reshape(10, 16, 256))

    for group in range(7):
        inside = bg[16 * group : 16 * group + 16, :, 128:384].reshape(256, 256)
        out = permuted("send_gx", inside)
        for b in range(4):
            rows = slice(16 * group, 16 * group + 16)
            for side in range(2):
                lanes = slice(128, 256) if side == 0 else slice(0, 128)
                face = out[64 * side + 16 * b : 64 * side + 16 * b + 16, lanes]
                ogx[side, b, rows] = face
                rgx[5 + b, side, rows] = face
    copies = halo_send(5, 0, lambda side, b: ogx[side, b], sgx, rgx)
    for group in range(7):
        at = slice(16 * group, 16 * group + 16)
        inside = bg[at, :, 128:384].reshape(256, 256)
        bg[at, :, 0:128] = permuted("low", inside[:, 128:256]).reshape(16, 16, 128)
        bg[at, :, 384:512] = permuted("high", inside[:, 0:128]).reshape(16, 16, 128)
    sum_send(2)
    gather_send(0)
    gather_send(1)
    halo = halo_recv(0, copies, rgx)
    for group in range(7):
        at = slice(16 * group, 16 * group + 16)
        rows = jnp.concatenate([halo[side][b][at] for side in range(2) for b in range(4)], axis=0)
        out = permuted("insert", rows)
        bg[at, :, 0:128] = bg[at, :, 0:128] + out[0:256].reshape(16, 16, 128)
        bg[at, :, 384:512] = bg[at, :, 384:512] + out[256:512].reshape(16, 16, 128)

    def backward(yq, carry):
        grad = jnp.zeros((256, 256), F32)
        for k9 in range(9):
            grad = grad + mm_nt(window(bg, 2 * yq + k9 // 3, k9 % 3, 8), wb[k9])
        out = permuted("swap", grad.astype(BF))
        for xq in range(4):
            for b in range(4):
                tile = out[16 * (4 * xq + b) : 16 * (4 * xq + b) + 16]
                for xl in range(2):
                    at = pl.ds(pl.multiple_of(64 * (2 * xq + xl) + 16 * yq, 16), 16)
                    dfeats_o[b, at, :] = tile[:, 128 * xl : 128 * xl + 128]
        return carry

    gather_send(2)
    lax.fori_loop(0, 4, backward, 0)
    for part in range(3):
        hand_over(part)
    for one in sent:
        one.wait_send()
    for part in range(3):
        finish(part)


def epilogue(norm, sums, pooled, dfeats, pooled_o, dfeats_o, conv_o, down_o, conv, down, sem):
    copies = [
        pltpu.make_async_copy(dfeats, dfeats_o, sem.at[0]),
        pltpu.make_async_copy(pooled, pooled_o, sem.at[1]),
    ]
    copies[0].start()
    copies[1].start()
    for part in range(3):
        conv[part] = (sums[part, 0:9].astype(F32) * norm).reshape(3, 3, 128, 128)
        one = pltpu.make_async_copy(conv.at[part], conv_o.at[:, part], sem.at[2 + part])
        one.start()
        copies.append(one)
    for tap in range(8):
        down[tap] = sums[tap // 3, 9 + tap % 3].astype(F32) * norm
    one = pltpu.make_async_copy(down, down_o, sem.at[5])
    one.start()
    copies.append(one)
    for one in copies:
        one.wait()


def per_device(feats, w_conv, w_down, cotangent, nbr_owner, nbr_slot):
    def buf(*shape, dtype=BF):
        return pltpu.VMEM(shape, dtype)

    def halo(rows, lanes, own=True):
        bufs = [buf(4, 2, rows, lanes), buf(9, 2, rows, lanes)]
        return ([buf(2, 4, rows, lanes)] if own else []) + bufs

    def in_hbm(value):
        return pltpu.with_memory_space_constraint(value, pltpu.HBM)

    vmem = pl.BlockSpec(memory_space=pltpu.VMEM)
    hbm = pl.BlockSpec(memory_space=pltpu.HBM)
    dma = pltpu.SemaphoreType.DMA
    operands = (
        feats[0], w_conv, w_down, cotangent[0], jnp.asarray(TABLES, BF), nbr_owner, nbr_slot
    )
    pooled, d_feats, sums = pl.pallas_call(
        kernel,
        out_shape=(
            pltpu.VMEM((4, 64, 128), BF),
            pltpu.VMEM((4, 512, 128), BF),
            pltpu.VMEM((3, 2, 48, 16, 128), BF),
        ),
        in_specs=[hbm] * 7,
        out_specs=(vmem, vmem, vmem),
        scratch_shapes=[
            buf(4, 512, 128), buf(27, 128, 128), buf(8, 128, 128), buf(4, 64, 128),
            buf(*TABLES.shape),
            pltpu.SMEM((1, 4, 6), jnp.int32), pltpu.SMEM((1, 4, 6), jnp.int32),
            buf(100, 16, 512), buf(112, 16, 512),
            buf(9, 512, 256), buf(9, 256, 512),
            buf(2, 8, 4, 16, 256, dtype=F32), buf(2, 8, 4, 16, 256),
            buf(4, 256, 256), buf(256, 128),
            buf(3, 2, 6, 128, 128, dtype=F32),
            *halo(64, 128, own=False), *halo(16, 128), *halo(48, 128),
            *halo(32, 256), *halo(32, 256),
            *halo(32, 256), *halo(48, 256), *halo(112, 128),
            buf(3, 768, 128), buf(3, 768, 128),
            buf(3, 48, 16, 128), buf(3, 48, 16, 128), buf(3, 96, 16, 128), buf(3, 6, 16, 128),
            dma((7,)),
            dma((8, 4)), dma((8, 4)),
            *([dma((3,))] * 10),
        ],
        compiler_params=pltpu.CompilerParams(
            collective_id=0, has_side_effects=True, vmem_limit_bytes=48 * 1024 * 1024
        ),
    )(*[in_hbm(one) for one in operands])
    norm = 1.0 / float(lax.axis_size("rep") * lax.axis_size("space") * 4 * 512) ** 0.5
    pooled, d_feats, conv, down = pl.pallas_call(
        functools.partial(epilogue, norm),
        out_shape=(
            jax.ShapeDtypeStruct((4, 64, 128), BF),
            jax.ShapeDtypeStruct((4, 512, 128), BF),
            jax.ShapeDtypeStruct((3, 3, 3, 128, 128), F32),
            jax.ShapeDtypeStruct((8, 128, 128), F32),
        ),
        in_specs=[vmem] * 3,
        out_specs=[hbm] * 4,
        scratch_shapes=[buf(3, 3, 3, 128, 128, dtype=F32), buf(8, 128, 128, dtype=F32), dma((6,))],
        compiler_params=pltpu.CompilerParams(vmem_limit_bytes=24 * 1024 * 1024),
    )(sums.reshape(3, 12, 128, 128), pooled, d_feats)
    return (pooled[None], d_feats[None], conv.reshape(27, 128, 128), down)


def solution(mesh):
    placed = (
        P("rep", "space", None, None),
        P(),
        P(),
        P("rep", "space", None, None),
        P("rep", "space", None),
        P("rep", "space", None),
    )
    return jax.shard_map(
        per_device,
        mesh=mesh,
        in_specs=placed,
        out_specs=(P("rep", "space", None, None), P("rep", "space", None, None), P(), P()),
        check_vma=False,
    )
```

```python
import functools

import jax
import jax.numpy as jnp
import numpy as np
from jax import lax
from jax.experimental import pallas as pl
from jax.experimental.pallas import tpu as pltpu
from jax.sharding import PartitionSpec as P

BF = jnp.bfloat16
F32 = jnp.float32
MESH = pl.DeviceIdType.MESH
SHIFTS = (-2, -1, 1, 2)
N_SPACE = 64
N_PLANE = 16
N_Z = 8


def onehot_tables():
    tables = {}

    def table(name, rows, cols):
        tables[name] = np.zeros((rows, cols), np.float32)
        return tables[name]

    swap = table("swap", 256, 256)
    for p in range(16):
        for q in range(16):
            swap[p * 16 + q, q * 16 + p] = 1
    send_y, recv_y = table("send_y", 128, 256), table("recv_y", 256, 384)
    wide, recv_z = np.zeros((768, 768), np.float32), table("recv_z", 384, 512)
    send_z, send_gr = wide[0:384], wide[384:768]
    move, back = table("move", 128, 128), table("back", 128, 128)
    send_gy, recv_gy = table("send_gy", 128, 512), table("recv_gy", 64, 128)
    send_gx = table("send_gx", 128, 256)
    low, high = table("low", 256, 256), table("high", 256, 256)
    insert = table("insert", 512, 128)
    for b in range(4):
        for xq in range(4):
            row = xq * 4 + b
            for z in range(8):
                at = z * 16 + row
                recv_y[at, 128 + at - 4 if xq > 0 else 256 + b * 16 + z] = 1
                recv_y[128 + at, at + 4 if xq < 3 else 264 + b * 16 + z] = 1
                move[b * 32 + z * 4 + xq, at] = 1
                back[at, b * 32 + z * 4 + xq] = 1
            for y in range(10):
                at = y * 16 + row

                def near(s, column):
                    if 1 <= y <= 8:
                        return (s - 1) * 128 + (y - 1) * 16 + column * 4 + b
                    return 276 + b * 48 + ((y > 0) * 2 + s - 1) * 4 + column

                recv_z[at, near(2, xq - 1) if xq > 0 else 256 + b * 48 + y] = 1
                recv_z[160 + at, near(1, xq + 1) if xq < 3 else 266 + b * 48 + y] = 1
                if y in (0, 9):
                    for s in (1, 2):
                        edge = 288 + 32 * s + (y > 0) * 16 + row
                        recv_z[edge, near(s, xq)] = 1
                        cell = 20 + ((y > 0) * 2 + s - 1) * 4 + xq
                        for side in range(2):
                            tile = 32 + (side * 2 + (y > 0)) * 2 + s - 1
                            send_z[side * 192 + b * 48 + cell, tile * 16 + row] = 1
            for k in range(16):
                if xq >= 1:
                    low[k * 16 + row, k * 16 + row - 4] = 1
                if xq <= 2:
                    high[k * 16 + row, k * 16 + row + 4] = 1
        for side in range(2):
            for zs in range(2):
                for xl in range(2):
                    for xq in range(4):
                        cell = b * 16 + zs * 8 + xl * 4 + xq
                        at = side * 256 + ((zs * 4 + b) * 2 + xl) * 16 + 12 - 12 * side + xq
                        send_gy[side * 64 + cell, at] = 1
                        recv_gy[xl * 32 + zs * 16 + xq * 4 + b, cell] = 1
            to, xq = side * 192 + b * 48, 3 - 3 * side
            for edge in range(2):
                for i in range(8):
                    send_gr[to + edge * 10 + 1 + i, edge * 128 + i * 16 + xq * 4 + b] = 1
                    send_gr[to + 20 + edge * 8 + i, 256 + edge * 128 + i * 16 + xq * 4 + b] = 1
                for zs in range(2):
                    at = 512 + (edge * 4 + b) * 16 + zs * 8 + 4 - 4 * side + xq
                    send_gr[to + edge * 10 + 9 * zs, at] = 1
            for end in range(2):
                to = side * 192 + b * 48 + end * 10
                for z in range(8):
                    at = side * 128 + (end * 4 + b) * 16 + 8 - 8 * side + z
                    send_y[side * 64 + b * 16 + end * 8 + z, at] = 1
                    send_z[to + 1 + z, (end * 4 + b) * 64 + z * 8 + 7 - 7 * side] = 1
                for edge in range(2):
                    at = 640 + (edge * 4 + b) * 16 + end * 8 + 7 - 7 * side
                    send_z[to + 9 * edge, at] = 1
        for k in range(16):
            send_gx[b * 16 + k, k * 16 + 12 + b] = 1
            send_gx[64 + b * 16 + k, k * 16 + b] = 1
            insert[k * 16 + b, b * 16 + k] = 1
            insert[256 + k * 16 + 12 + b, 64 + b * 16 + k] = 1
    places, parts, start = {}, [], 0
    for name, value in tables.items():
        rows, cols = value.shape
        places[name] = (start, rows, cols)
        parts.append(np.pad(value, ((0, 0), (0, 512 - cols))))
        start += rows
    return places, np.concatenate(parts), wide


PLACES, TABLES, WIDE = onehot_tables()


def mm(left, right):
    return jnp.dot(left, right, preferred_element_type=F32)


def mm_nt(left, right):
    return lax.dot_general(left, right, (((1,), (1,)), ((), ())), preferred_element_type=F32)


def kernel(
    feats_h, wc_h, wd_h, cot_h, tab_h, wide_h, own_h, slot_h,
    pooled_o, dfeats_o, sums_o,
    feats, wc, wd, cot, tab, wide, own_s, slot_s, bf, bg, wf, wb, gh, hid, gpt, cotp, dwf,
    sx, rx, oy, sy, ry, oz, sz, rz, oyi, syi, ryi, ozi, szi, rzi, ogz, sgz, rgz, ogy, sgy, rgy, ogx, sgx, rgx,
    ogyi, sgyi, rgyi, ogxi, sgxi, rgxi,
    s1, r1, s2, r2, r3, fin,
    lsem, hs, hr, cs, cr, xs, xr, vs, vr, as_, ar, fs, fr,
):
    pos = lax.axis_index("space")
    rep = lax.axis_index("rep")
    core = lax.rem(pos, 2)
    zpos = lax.rem(lax.div(pos, 2), 8)
    xpos = lax.div(pos, 16)
    plane = xpos * 4 + rep
    sibling = pos + 1 - 2 * core

    def in_space(to):
        return {"space": to, "rep": rep}

    def in_plane(k):
        to = lax.rem(plane + k, N_PLANE)
        return {"space": lax.div(to, 4) * 16 + lax.rem(pos, 16), "rep": lax.rem(to, 4)}

    def in_z(k):
        to = lax.rem(zpos + k, N_Z)
        return {"space": xpos * 16 + to * 2 + core, "rep": rep}

    loads = [
        pltpu.make_async_copy(src, dst, lsem.at[i])
        for i, (src, dst) in enumerate(
            (
                (own_h, own_s), (slot_h, slot_s), (feats_h, feats), (tab_h, tab),
                (cot_h, cot), (wc_h, wc), (wd_h, wd), (wide_h, wide),
            )
        )
    ]
    for one in loads:
        one.start()

    barrier = pltpu.get_barrier_semaphore()
    for t in SHIFTS:
        to = lax.rem(pos + t + N_SPACE, N_SPACE)
        pl.semaphore_signal(barrier, inc=1, device_id=in_space(to), device_id_type=MESH)
    pl.semaphore_signal(barrier, inc=1, device_id=in_space(sibling), device_id_type=MESH)

    def greet_plane(k, carry):
        pl.semaphore_signal(barrier, inc=1, device_id=in_plane(k), device_id_type=MESH)
        return carry

    def greet_z(k, carry):
        pl.semaphore_signal(barrier, inc=1, device_id=in_z(k), device_id_type=MESH)
        return carry

    lax.fori_loop(1, N_PLANE, greet_plane, 0)
    lax.fori_loop(1, N_Z, greet_z, 0)

    loads[0].wait()
    loads[1].wait()

    owners = [[own_s[0, b, d] for d in range(6)] for b in range(4)]
    slots = [[slot_s[0, b, d] for d in range(6)] for b in range(4)]

    def pick(d, t):
        found = jnp.int32(0)
        for b in range(1, 4):
            hit = (owners[b][d] == pos + t) & (owners[b][d] >= 0)
            found = jnp.where(hit, b, found)
        return found

    def place(d, b):
        gap = pos - owners[b][d]
        far = jnp.clip(jnp.where(gap < 0, gap + 2, gap + 1), 0, 3)
        near = jnp.clip(5 + slots[b][d], 5, 8)
        return jnp.where(owners[b][d] < 0, 4, jnp.where(gap == 0, near, far))

    for ref in (rx, ry, rz, ryi, rzi, rgz, rgy, rgx, rgyi, rgxi):
        ref[4] = jnp.zeros(ref.shape[1:], BF)

    def halo_copy(phase, i, send, recv):
        to = lax.rem(pos + SHIFTS[i] + N_SPACE, N_SPACE)
        return pltpu.make_async_remote_copy(
            src_ref=send.at[i],
            dst_ref=recv.at[i],
            send_sem=hs.at[phase, i],
            recv_sem=hr.at[phase, i],
            device_id=in_space(to),
            device_id_type=MESH,
        )

    sent = []

    def halo_send(phase, axis, own, send, recv):
        copies = []
        for i, t in enumerate(SHIFTS):
            for side in range(2):
                send[i, side] = own(side, pick(2 * axis + side, t))
            one = halo_copy(phase, i, send, recv)
            one.start()
            copies.append(one)
        sent.extend(copies)
        return copies

    def halo_recv(axis, copies, recv):
        for one in copies:
            one.wait_recv()
        return [
            [recv[place(2 * axis + 1 - side, b), side] for b in range(4)] for side in range(2)
        ]

    def onehot(name):
        start, rows, cols = PLACES[name]
        return tab[start : start + rows, 0:cols]

    def permuted(name, value):
        return mm(onehot(name), value).astype(BF)

    loads[2].wait()
    for b in range(4):
        rx[5 + b, 0] = feats[b, 448:512, :]
        rx[5 + b, 1] = feats[b, 0:64, :]
    for side in range(2):
        for i, t in enumerate(SHIFTS):
            rows = slice(448, 512) if side == 0 else slice(0, 64)
            sx[i, side] = feats[pick(side, t), rows, :]
    pl.semaphore_wait(barrier, 4 + 1 + N_PLANE - 1 + N_Z - 1)
    copies = [halo_copy(0, i, sx, rx) for i in range(4)]
    for one in copies:
        one.start()
    sent.extend(copies)

    loads[3].wait()

    def x_layer(s, chunk, halo):
        rows = []
        for xq in range(4):
            x = 2 * xq + s - 1
            for b in range(4):
                if x < 0 or x > 7:
                    rows.append(halo[0 if x < 0 else 1][b][16 * chunk : 16 * chunk + 16])
                else:
                    rows.append(feats[b, 64 * x + 16 * chunk : 64 * x + 16 * chunk + 16, :])
        return jnp.concatenate(rows, axis=0)

    def put_rows(ref, y, z, count, lanes, value):
        ref[pl.ds(y * 10 + z, count), :, lanes] = value

    for chunk in range(4):
        both = jnp.concatenate([x_layer(1, chunk, None), x_layer(2, chunk, None)], axis=1)
        out = permuted("swap", both).reshape(2, 8, 16, 256)
        for j in range(2):
            put_rows(bf, 2 * chunk + j + 1, 1, 8, slice(128, 384), out[j])

    def inner_faces(ref, at, own, recv):
        for side in range(2):
            flat = jnp.concatenate([ref[i, :, 128:384] for i in at(side)], axis=0)
            faces = permuted("move", flat).reshape(4, 32, 256)
            own[side] = faces
            recv[5:9, side] = faces

    inner_faces(bf, lambda side: [(8 - 7 * side) * 10 + z for z in range(1, 9)], oyi, ryi)
    copies_y = halo_send(6, 1, lambda side, b: oyi[side, b], syi, ryi)
    inner_faces(bf, lambda side: [y * 10 + 8 - 7 * side for y in range(1, 9)], ozi, rzi)
    copies_z = halo_send(7, 2, lambda side, b: ozi[side, b], szi, rzi)

    halo = halo_recv(0, copies, rx)
    def rim_faces(out, count, own, recv):
        faces = out.astype(BF).reshape(2, 4, count, 128)
        for side in range(2):
            own[side] = faces[side]
            recv[5:9, side] = faces[side]

    ends = [[halo[end][b][rows] for end in range(2) for b in range(4)]
            for rows in (slice(48, 64), slice(0, 16))]
    rim_faces(mm(onehot("send_y"), jnp.concatenate(ends[0] + ends[1], axis=0)), 16, oy, ry)
    copies = halo_send(1, 1, lambda side, b: oy[side, b], sy, ry)
    x_halo = [halo[end][b] for end in range(2) for b in range(4)]

    for chunk in range(4):
        both = jnp.concatenate([x_layer(0, chunk, halo), x_layer(3, chunk, halo)], axis=1)
        out = permuted("swap", both).reshape(2, 8, 16, 256)
        for j in range(2):
            put_rows(bf, 2 * chunk + j + 1, 1, 8, slice(0, 128), out[j, :, :, 0:128])
            put_rows(bf, 2 * chunk + j + 1, 1, 8, slice(384, 512), out[j, :, :, 128:256])

    for one in loads[4:]:
        one.wait()
    cot_rows = jnp.concatenate(
        [cot[b, 16 * xq : 16 * xq + 16, :] for xq in range(4) for b in range(4)], axis=0
    )
    cot_perm = permuted("swap", cot_rows)
    cotp[...] = cot_perm

    def down_weight(j, k):
        return jnp.concatenate([wd[2 * j + k], wd[4 + 2 * j + k]], axis=0)

    for j in range(2):
        for k in range(2):
            out = mm_nt(cot_perm, down_weight(j, k)).reshape(4, 4, 16, 256)
            for zq in range(4):
                gh[j, 2 * zq + k] = out[:, zq]

    def weights(k9, carry):
        for s in range(4):
            for xl in range(2):
                dx = s - xl
                fwd_at = (pl.ds(s * 128, 128), pl.ds(xl * 128, 128))
                bwd_at = (pl.ds(xl * 128, 128), pl.ds(s * 128, 128))
                if 0 <= dx <= 2:
                    wf[(k9,) + fwd_at] = wc[9 * dx + k9]
                    wb[(k9,) + bwd_at] = wc[9 * (2 - dx) + 8 - k9]
                else:
                    wf[(k9,) + fwd_at] = jnp.zeros((128, 128), BF)
                    wb[(k9,) + bwd_at] = jnp.zeros((128, 128), BF)
        return carry

    lax.fori_loop(0, 9, weights, 0)

    def both_sides(make):
        return jnp.concatenate([make(0), make(1)], axis=1)

    def inner_halo(axis, copies, recv):
        halo = halo_recv(axis, copies, recv)
        return [permuted("back", jnp.concatenate(halo[side], axis=0)) for side in range(2)]

    def rim_rows(inside, halo, rows):
        def one(side):
            pad = jnp.zeros((rows - 256 - 4 * halo[side][0].shape[0], 128), BF)
            parts = [inside[side][:, 0:128], inside[side][:, 128:256], *halo[side], pad]
            return jnp.concatenate(parts, axis=0)

        return both_sides(one)

    inside = inner_halo(1, copies_y, ryi)
    for side in range(2):
        put_rows(bf, 9 * side, 1, 8, slice(128, 384), inside[side].reshape(8, 16, 256))
    corner_tiles = [
        inside[edge][16 * z : 16 * z + 16, 128 * s : 128 * s + 128]
        for z in (7, 0) for edge in range(2) for s in range(2)
    ]
    early = mm(wide[0:384, 0:640], jnp.concatenate(x_halo + corner_tiles, axis=0))
    halo = halo_recv(1, copies, ry)

    late = jnp.concatenate([halo[side][b] for side in range(2) for b in range(4)], axis=0)
    rim_faces(early + mm(wide[0:384, 640:768], late), 48, oz, rz)
    copies = halo_send(2, 2, lambda side, b: oz[side, b], sz, rz)
    out = permuted("recv_y", rim_rows(inside, halo, 384)).reshape(2, 8, 16, 256)
    for side in range(2):
        lanes = slice(128 * side, 128 * side + 128)
        put_rows(bf, 9 * side, 1, 8, slice(0, 128), out[0, :, :, lanes])
        put_rows(bf, 9 * side, 1, 8, slice(384, 512), out[1, :, :, lanes])

    inside = inner_halo(2, copies_z, rzi)
    for side in range(2):
        for y in range(1, 9):
            bf[y * 10 + 9 * side, :, 128:384] = inside[side][16 * y - 16 : 16 * y]
    bg[100:112] = jnp.zeros((12, 16, 512), BF)
    dwf[2, 1, 5] = jnp.zeros((128, 128), F32)
    def window(ref, y, z, count):
        lower = ref[pl.ds(y * 10 + z, count)]
        upper = ref[pl.ds(y * 10 + 10 + z, count)]
        return jnp.concatenate([lower, upper], axis=0).reshape(32 * count, 512)

    def activate(pre, grad):
        sig = 1.0 / (1.0 + jnp.exp(-pre))
        hidden = (pre * sig).astype(BF).reshape(-1, 16, 256)
        grad = (grad * sig * (1.0 + pre * (1.0 - sig))).astype(BF)
        return hidden, grad.reshape(-1, 16, 256)

    def inner(yq, carry):
        pre = jnp.zeros((192, 256), F32)
        for k9 in range(9):
            pre = pre + mm(window(bf, 2 * yq + k9 // 3, 1 + k9 % 3, 6), wf[k9])
        grad = jnp.concatenate([gh[j, 1:7, yq] for j in range(2)], axis=0).reshape(192, 256)
        hidden, grad = activate(pre, grad)
        for j in range(2):
            hid[j, 1:7, yq] = hidden[6 * j : 6 * j + 6]
            bg[pl.ds((2 * yq + j + 1) * 10 + 2, 6), :, 128:384] = grad[6 * j : 6 * j + 6]
        return carry

    lax.fori_loop(0, 4, inner, 0)

    middle = [(y, z) for y in range(8) for z in range(1, 7)]
    outer = [(y, z) for y in range(8) for z in (0, 7)]
    groups = [middle[0:16], middle[16:32], middle[32:48], outer]

    def tiles(ref, group, dy, dz):
        return jnp.concatenate([ref[(y + dy) * 10 + z + dz] for y, z in group], axis=0)

    def turn(at):
        gpt[at] = tiles(bg, groups[at], 1, 1)[:, 128:384].astype(F32).T.astype(BF)

    def grad_conv(part, chosen, last):
        for dz in range(3):
            first = jnp.zeros((256, 256), F32)
            second = jnp.zeros((256, 256), F32)
            for at in chosen:
                rows = tiles(bf, groups[at], part, dz)
                first = first + mm(gpt[at], rows[:, 0:256])
                second = second + mm(gpt[at], rows[:, 256:512])
            taps = (
                first[0:128, 0:128] + first[128:256, 128:256],
                first[0:128, 128:256] + second[128:256, 0:128],
                second[0:128, 0:128] + second[128:256, 128:256],
            )
            for dx in range(3):
                slot = dx * 3 + dz
                to = (part, slot // 6, slot % 6)
                dwf[to] = (dwf[to] + taps[dx]).T if last else taps[dx]

    for at in range(3):
        turn(at)
    for part in range(3):
        grad_conv(part, (0, 1, 2), False)

    halo = halo_recv(2, copies, rz)
    out = permuted("recv_z", rim_rows(inside, halo, 512)).reshape(24, 16, 256)
    for side in range(2):
        lanes = slice(128 * side, 128 * side + 128)
        for y in range(10):
            bf[y * 10 + 9 * side, :, 0:128] = out[y, :, lanes]
            bf[y * 10 + 9 * side, :, 384:512] = out[10 + y, :, lanes]
        for i, y in enumerate((0, 9)):
            bf[y * 10 + 9 * side, :, 128:256] = out[20 + i, :, lanes]
            bf[y * 10 + 9 * side, :, 256:384] = out[22 + i, :, lanes]

    pre = jnp.zeros((256, 256), F32)
    for k9 in range(9):
        pre = pre + mm(tiles(bf, outer, k9 // 3, k9 % 3), wf[k9])
    grad = jnp.concatenate([gh[y % 2, z, y // 2] for y, z in outer], axis=0)
    hidden, grad = activate(pre, grad)
    for at, (y, z) in enumerate(outer):
        hid[y % 2, z, y // 2] = hidden[at]
        bg[(y + 1) * 10 + z + 1, :, 128:384] = grad[at]

    for side in range(2):
        z = 8 if side == 0 else 1
        flat = jnp.concatenate([bg[y * 10 + z, :, 128:384] for y in range(1, 9)], axis=0)
        faces = permuted("move", flat).reshape(4, 32, 256)
        ogz[side] = faces
        rgz[5:9, side] = faces
    copies = halo_send(3, 2, lambda side, b: ogz[side, b], sgz, rgz)

    def core_copy(part):
        return pltpu.make_async_remote_copy(
            src_ref=s1.at[part], dst_ref=r1.at[part], send_sem=cs.at[part], recv_sem=cr.at[part],
            device_id=in_space(sibling), device_id_type=MESH,
        )

    def core_send(part):
        s1[part] = dwf[part, 1 - core].reshape(768, 128).astype(BF)
        core_copy(part).start()

    def each(count, act):
        def body(k, carry):
            act(k)
            return carry

        lax.fori_loop(1, count, body, 0)

    plane_group, z_group = (N_PLANE, plane, in_plane), (N_Z, zpos, in_z)
    order = [(plane_group, z_group)] * 3

    def chunk(part, index):
        size = 48 // order[part][0][0]
        return pl.ds(index * size, size)

    def scatter_copy(part, k):
        count, mine, to = order[part][0]
        return pltpu.make_async_remote_copy(
            src_ref=s2.at[part, chunk(part, lax.rem(mine + k, count))],
            dst_ref=r2.at[part, chunk(part, mine)],
            send_sem=xs.at[part], recv_sem=xr.at[part],
            device_id=to(k), device_id_type=MESH,
        )

    def sum_copy(part, k):
        _, mine, to = order[part][1]
        block = r3.at[part, chunk(part, mine)]
        return pltpu.make_async_remote_copy(
            src_ref=block, dst_ref=block, send_sem=vs.at[part], recv_sem=vr.at[part],
            device_id=to(k), device_id_type=MESH,
        )

    def gather_copy(part, k):
        _, mine, to = order[part][0]
        return pltpu.make_async_remote_copy(
            src_ref=fin.at[part, chunk(part, 0)], dst_ref=sums_o.at[part, core, chunk(part, mine)],
            send_sem=as_.at[part], recv_sem=ar.at[part],
            device_id=to(k), device_id_type=MESH,
        )

    def hand_copy(part):
        half = sums_o.at[part, core]
        return pltpu.make_async_remote_copy(
            src_ref=half, dst_ref=half, send_sem=fs.at[part], recv_sem=fr.at[part],
            device_id=in_space(sibling), device_id_type=MESH,
        )

    def all_bytes(ref, sem):
        pltpu.make_async_copy(ref, ref, sem).wait()

    def sent_bytes(part, stage):
        size = 48 // order[part][0][0]
        return pl.ds(0, size * (order[part][stage][0] - 1))

    def added(ref, part, count):
        total = ref[part, chunk(part, 0)].astype(F32)
        for i in range(1, count):
            total = total + ref[part, chunk(part, i)].astype(F32)
        return total.astype(BF)

    def scatter_send(part):
        core_copy(part).wait_recv()
        mine = dwf[part, core].reshape(768, 128) + r1[part].astype(F32)
        s2[part] = mine.astype(BF).reshape(48, 16, 128)
        count, index, _ = order[part][0]
        each(count, lambda k: scatter_copy(part, k).start())
        r2[part, chunk(part, index)] = s2[part, chunk(part, index)]

    def sum_send(part):
        all_bytes(r2.at[part, sent_bytes(part, 0)], xr.at[part])
        count, index, _ = order[part][1]
        r3[part, chunk(part, index)] = added(r2, part, order[part][0][0])
        each(count, lambda k: sum_copy(part, k).start())

    def gather_send(part):
        all_bytes(r3.at[part, sent_bytes(part, 1)], vr.at[part])
        count, index, _ = order[part][0]
        total = added(r3, part, order[part][1][0])
        fin[part, chunk(part, 0)] = total
        each(count, lambda k: gather_copy(part, k).start())
        sums_o[part, core, chunk(part, index)] = total

    def hand_over(part):
        all_bytes(sums_o.at[part, core, sent_bytes(part, 0)], ar.at[part])
        hand_copy(part).start()

    def finish(part):
        hand_copy(part).wait_recv()
        core_copy(part).wait_send()
        all_bytes(s2.at[part, sent_bytes(part, 0)], xs.at[part])
        all_bytes(r3.at[part, sent_bytes(part, 1)], vs.at[part])
        all_bytes(sums_o.at[part, core, sent_bytes(part, 0)], as_.at[part])
        hand_copy(part).wait_send()

    def down_rows(j, k):
        tiles = [hid[j, 2 * zq + k, yq] for yq in range(4) for zq in range(4)]
        return jnp.concatenate(tiles, axis=0)

    cot_t = cotp[...].astype(F32).T.astype(BF)
    for j in range(2):
        for k in range(2):
            out = mm(cot_t, down_rows(j, k))
            for i in range(2):
                tap = 4 * i + 2 * j + k
                dwf[tap // 3, 1, 3 + tap % 3] = out[:, 128 * i : 128 * i + 128].T
    turn(3)
    for part in range(3):
        grad_conv(part, (3,), True)
        core_send(part)

    inner_faces(bg, lambda side: [(8 - 7 * side) * 10 + z for z in range(1, 9)], ogyi, rgyi)
    copies_y = halo_send(8, 1, lambda side, b: ogyi[side, b], sgyi, rgyi)
    within = [y * 10 + z for y in range(1, 9) for z in range(1, 9)]
    rim = [*range(0, 10), *range(90, 100), *range(10, 90, 10), *range(19, 90, 10)]
    rim += list(range(100, 112))

    def inside_rows(group):
        return jnp.concatenate([bg[i, :, 128:384] for i in group], axis=0)

    for group in range(4):
        rows = slice(16 * group, 16 * group + 16)
        out = permuted("send_gx", inside_rows(within[rows]))
        for b in range(4):
            for side in range(2):
                lanes = slice(128, 256) if side == 0 else slice(0, 128)
                face = out[64 * side + 16 * b : 64 * side + 16 * b + 16, lanes]
                ogxi[side, b, rows] = face
                rgxi[5 + b, side, rows] = face
    copies_x = halo_send(9, 0, lambda side, b: ogxi[side, b], sgxi, rgxi)

    for part in range(3):
        scatter_send(part)

    halo = halo_recv(2, copies, rgz)
    ends = [
        halo[zs][b][rows, 128 * xl : 128 * xl + 128]
        for rows in (slice(16, 32), slice(0, 16))
        for zs in range(2) for b in range(4) for xl in range(2)
    ]
    rim_faces(mm(onehot("send_gy"), jnp.concatenate(ends, axis=0)), 16, ogy, rgy)
    copies = halo_send(4, 1, lambda side, b: ogy[side, b], sgy, rgy)
    inside_z = [permuted("back", jnp.concatenate(halo[zs], axis=0)) for zs in range(2)]
    inside_y = inner_halo(1, copies_y, rgyi)
    for side in range(2):
        for y in range(1, 9):
            bg[y * 10 + 9 * side, :, 128:384] = inside_z[side][16 * y - 16 : 16 * y]
        put_rows(bg, 9 * side, 1, 8, slice(128, 384), inside_y[side].reshape(8, 16, 256))
    early = mm(wide[384:768, 0:512], jnp.concatenate(inside_y + inside_z, axis=0))

    def shift_rows(group):
        rows = inside_rows(group)
        lower = permuted("low", rows[:, 128:256]).reshape(16, 16, 128)
        upper = permuted("high", rows[:, 0:128]).reshape(16, 16, 128)
        for at, i in enumerate(group):
            bg[i, :, 0:128] = lower[at]
            bg[i, :, 384:512] = upper[at]

    def insert_rows(group, halo, rows):
        layers = [halo[side][b][rows] for side in range(2) for b in range(4)]
        out = permuted("insert", jnp.concatenate(layers, axis=0)).reshape(32, 16, 128)
        for at, i in enumerate(group):
            bg[i, :, 0:128] = bg[i, :, 0:128] + out[at]
            bg[i, :, 384:512] = bg[i, :, 384:512] + out[16 + at]

    for group in range(4):
        shift_rows(within[16 * group : 16 * group + 16])
    total = jnp.zeros((256, 128), F32)
    for j in range(2):
        for k in range(2):
            total = total + mm(down_rows(j, k), down_weight(j, k))
    out = permuted("swap", total.astype(BF))
    for b in range(4):
        for xq in range(4):
            at = 16 * (4 * xq + b)
            pooled_o[b, 16 * xq : 16 * xq + 16, :] = out[at : at + 16]
    sum_send(0)
    sum_send(1)
    halo = halo_recv(1, copies, rgy)
    late = jnp.concatenate([halo[side][b] for side in range(2) for b in range(4)], axis=0)
    late = mm(wide[384:768, 512:640], late)
    faces = (early[0:192, 128:256] + late[0:192], early[192:384, 0:128] + late[192:384])
    rim_faces(jnp.concatenate(faces, axis=0), 48, ogx, rgx)
    copies = halo_send(5, 0, lambda side, b: ogx[side, b], sgx, rgx)
    corners = both_sides(lambda side: jnp.concatenate(halo[side], axis=0))
    corners = jnp.concatenate([corners, jnp.zeros((64, 256), BF)], axis=0)
    out = permuted("recv_gy", corners).reshape(2, 2, 16, 256)
    for side in range(2):
        for zs in range(2):
            for xl in range(2):
                lanes = slice(128 + 128 * xl, 256 + 128 * xl)
                face = out[xl, zs, :, 128 * side : 128 * side + 128]
                bg[90 * side + 9 * zs, :, lanes] = face
    for group in range(3):
        shift_rows(rim[16 * group : 16 * group + 16])
    sum_send(2)
    halo = halo_recv(0, copies_x, rgxi)
    for group in range(4):
        rows = slice(16 * group, 16 * group + 16)
        insert_rows(within[rows], halo, rows)
    gather_send(0)
    gather_send(1)
    halo = halo_recv(0, copies, rgx)
    for group in range(3):
        rows = slice(16 * group, 16 * group + 16)
        insert_rows(rim[rows], halo, rows)

    def backward(yq, carry):
        grad = jnp.zeros((256, 256), F32)
        for k9 in range(9):
            grad = grad + mm_nt(window(bg, 2 * yq + k9 // 3, k9 % 3, 8), wb[k9])
        out = permuted("swap", grad.astype(BF))
        for xq in range(4):
            for b in range(4):
                tile = out[16 * (4 * xq + b) : 16 * (4 * xq + b) + 16]
                for xl in range(2):
                    at = pl.ds(pl.multiple_of(64 * (2 * xq + xl) + 16 * yq, 16), 16)
                    dfeats_o[b, at, :] = tile[:, 128 * xl : 128 * xl + 128]
        return carry

    gather_send(2)
    lax.fori_loop(0, 4, backward, 0)
    for part in range(3):
        hand_over(part)
    for one in sent:
        one.wait_send()
    for part in range(3):
        finish(part)


def epilogue(norm, sums, pooled, dfeats, pooled_o, dfeats_o, conv_o, down_o, conv, down, sem):
    copies = [
        pltpu.make_async_copy(dfeats, dfeats_o, sem.at[0]),
        pltpu.make_async_copy(pooled, pooled_o, sem.at[1]),
    ]
    copies[0].start()
    copies[1].start()
    for part in range(3):
        conv[part] = (sums[part, 0:9].astype(F32) * norm).reshape(3, 3, 128, 128)
        one = pltpu.make_async_copy(conv.at[part], conv_o.at[:, part], sem.at[2 + part])
        one.start()
        copies.append(one)
    for tap in range(8):
        down[tap] = sums[tap // 3, 9 + tap % 3].astype(F32) * norm
    one = pltpu.make_async_copy(down, down_o, sem.at[5])
    one.start()
    copies.append(one)
    for one in copies:
        one.wait()


def per_device(feats, w_conv, w_down, cotangent, nbr_owner, nbr_slot):
    def buf(*shape, dtype=BF):
        return pltpu.VMEM(shape, dtype)

    def halo(rows, lanes, own=True):
        bufs = [buf(4, 2, rows, lanes), buf(9, 2, rows, lanes)]
        return ([buf(2, 4, rows, lanes)] if own else []) + bufs

    def in_hbm(value):
        return pltpu.with_memory_space_constraint(value, pltpu.HBM)

    vmem = pl.BlockSpec(memory_space=pltpu.VMEM)
    hbm = pl.BlockSpec(memory_space=pltpu.HBM)
    dma = pltpu.SemaphoreType.DMA
    operands = (
        feats[0], w_conv, w_down, cotangent[0], jnp.asarray(TABLES, BF), jnp.asarray(WIDE, BF),
        nbr_owner, nbr_slot,
    )
    pooled, d_feats, sums = pl.pallas_call(
        kernel,
        out_shape=(
            pltpu.VMEM((4, 64, 128), BF),
            pltpu.VMEM((4, 512, 128), BF),
            pltpu.VMEM((3, 2, 48, 16, 128), BF),
        ),
        in_specs=[hbm] * 8,
        out_specs=(vmem, vmem, vmem),
        scratch_shapes=[
            buf(4, 512, 128), buf(27, 128, 128), buf(8, 128, 128), buf(4, 64, 128),
            buf(*TABLES.shape), buf(*WIDE.shape),
            pltpu.SMEM((1, 4, 6), jnp.int32), pltpu.SMEM((1, 4, 6), jnp.int32),
            buf(100, 16, 512), buf(112, 16, 512),
            buf(9, 512, 256), buf(9, 256, 512),
            buf(2, 8, 4, 16, 256, dtype=F32), buf(2, 8, 4, 16, 256),
            buf(4, 256, 256), buf(256, 128),
            buf(3, 2, 6, 128, 128, dtype=F32),
            *halo(64, 128, own=False), *halo(16, 128), *halo(48, 128),
            *halo(32, 256), *halo(32, 256),
            *halo(32, 256), *halo(16, 128), *halo(48, 128),
            *halo(32, 256), *halo(64, 128),
            buf(3, 768, 128), buf(3, 768, 128),
            buf(3, 48, 16, 128), buf(3, 48, 16, 128), buf(3, 96, 16, 128), buf(3, 6, 16, 128),
            dma((8,)),
            dma((10, 4)), dma((10, 4)),
            *([dma((3,))] * 10),
        ],
        compiler_params=pltpu.CompilerParams(
            collective_id=0, has_side_effects=True, vmem_limit_bytes=48 * 1024 * 1024
        ),
    )(*[in_hbm(one) for one in operands])
    norm = 1.0 / float(lax.axis_size("rep") * lax.axis_size("space") * 4 * 512) ** 0.5
    pooled, d_feats, conv, down = pl.pallas_call(
        functools.partial(epilogue, norm),
        out_shape=(
            jax.ShapeDtypeStruct((4, 64, 128), BF),
            jax.ShapeDtypeStruct((4, 512, 128), BF),
            jax.ShapeDtypeStruct((3, 3, 3, 128, 128), F32),
            jax.ShapeDtypeStruct((8, 128, 128), F32),
        ),
        in_specs=[vmem] * 3,
        out_specs=[hbm] * 4,
        scratch_shapes=[buf(3, 3, 3, 128, 128, dtype=F32), buf(8, 128, 128, dtype=F32), dma((6,))],
        compiler_params=pltpu.CompilerParams(vmem_limit_bytes=24 * 1024 * 1024),
    )(sums.reshape(3, 12, 128, 128), pooled, d_feats)
    return (pooled[None], d_feats[None], conv.reshape(27, 128, 128), down)


def solution(mesh):
    placed = (
        P("rep", "space", None, None),
        P(),
        P(),
        P("rep", "space", None, None),
        P("rep", "space", None),
        P("rep", "space", None),
    )
    return jax.shard_map(
        per_device,
        mesh=mesh,
        in_specs=placed,
        out_specs=(P("rep", "space", None, None), P("rep", "space", None, None), P(), P()),
        check_vma=False,
    )
```

```python
import functools

import jax
import jax.numpy as jnp
import numpy as np
from jax import lax
from jax.experimental import pallas as pl
from jax.experimental.pallas import tpu as pltpu
from jax.sharding import PartitionSpec as P

BF = jnp.bfloat16
F32 = jnp.float32
MESH = pl.DeviceIdType.MESH
SHIFTS = (-2, -1, 1, 2)
N_SPACE = 64
N_PLANE = 16
N_Z = 8


def onehot_tables():
    tables = {}

    def table(name, rows, cols):
        tables[name] = np.zeros((rows, cols), np.float32)
        return tables[name]

    swap = table("swap", 256, 256)
    for p in range(16):
        for q in range(16):
            swap[p * 16 + q, q * 16 + p] = 1
    send_y, recv_y = table("send_y", 128, 256), table("recv_y", 256, 384)
    wide, recv_z = np.zeros((768, 768), np.float32), table("recv_z", 384, 512)
    send_z, send_gr = wide[0:384], wide[384:768]
    move, back = table("move", 128, 128), table("back", 128, 128)
    send_gy, recv_gy = table("send_gy", 128, 512), table("recv_gy", 64, 128)
    send_gx = table("send_gx", 128, 256)
    low, high = table("low", 256, 256), table("high", 256, 256)
    insert = table("insert", 512, 128)
    for b in range(4):
        for xq in range(4):
            row = xq * 4 + b
            for z in range(8):
                at = z * 16 + row
                recv_y[at, 128 + at - 4 if xq > 0 else 256 + b * 16 + z] = 1
                recv_y[128 + at, at + 4 if xq < 3 else 264 + b * 16 + z] = 1
                move[b * 32 + z * 4 + xq, at] = 1
                back[at, b * 32 + z * 4 + xq] = 1
            for y in range(10):
                at = y * 16 + row

                def near(s, column):
                    if 1 <= y <= 8:
                        return (s - 1) * 128 + (y - 1) * 16 + column * 4 + b
                    return 276 + b * 48 + ((y > 0) * 2 + s - 1) * 4 + column

                recv_z[at, near(2, xq - 1) if xq > 0 else 256 + b * 48 + y] = 1
                recv_z[160 + at, near(1, xq + 1) if xq < 3 else 266 + b * 48 + y] = 1
                if y in (0, 9):
                    for s in (1, 2):
                        edge = 288 + 32 * s + (y > 0) * 16 + row
                        recv_z[edge, near(s, xq)] = 1
                        cell = 20 + ((y > 0) * 2 + s - 1) * 4 + xq
                        for side in range(2):
                            tile = 32 + (side * 2 + (y > 0)) * 2 + s - 1
                            send_z[side * 192 + b * 48 + cell, tile * 16 + row] = 1
            for k in range(16):
                if xq >= 1:
                    low[k * 16 + row, k * 16 + row - 4] = 1
                if xq <= 2:
                    high[k * 16 + row, k * 16 + row + 4] = 1
        for side in range(2):
            for zs in range(2):
                for xl in range(2):
                    for xq in range(4):
                        cell = b * 16 + zs * 8 + xl * 4 + xq
                        at = side * 256 + ((zs * 4 + b) * 2 + xl) * 16 + 12 - 12 * side + xq
                        send_gy[side * 64 + cell, at] = 1
                        recv_gy[xl * 32 + zs * 16 + xq * 4 + b, cell] = 1
            to, xq = side * 192 + b * 48, 3 - 3 * side
            for edge in range(2):
                for i in range(8):
                    send_gr[to + edge * 10 + 1 + i, edge * 128 + i * 16 + xq * 4 + b] = 1
                    send_gr[to + 20 + edge * 8 + i, 256 + edge * 128 + i * 16 + xq * 4 + b] = 1
                for zs in range(2):
                    at = 512 + (edge * 4 + b) * 16 + zs * 8 + 4 - 4 * side + xq
                    send_gr[to + edge * 10 + 9 * zs, at] = 1
            for end in range(2):
                to = side * 192 + b * 48 + end * 10
                for z in range(8):
                    at = side * 128 + (end * 4 + b) * 16 + 8 - 8 * side + z
                    send_y[side * 64 + b * 16 + end * 8 + z, at] = 1
                    send_z[to + 1 + z, (end * 4 + b) * 64 + z * 8 + 7 - 7 * side] = 1
                for edge in range(2):
                    at = 640 + (edge * 4 + b) * 16 + end * 8 + 7 - 7 * side
                    send_z[to + 9 * edge, at] = 1
        for k in range(16):
            send_gx[b * 16 + k, k * 16 + 12 + b] = 1
            send_gx[64 + b * 16 + k, k * 16 + b] = 1
            insert[k * 16 + b, b * 16 + k] = 1
            insert[256 + k * 16 + 12 + b, 64 + b * 16 + k] = 1
    places, parts, start = {}, [], 0
    for name, value in tables.items():
        rows, cols = value.shape
        places[name] = (start, rows, cols)
        parts.append(np.pad(value, ((0, 0), (0, 512 - cols))))
        start += rows
    return places, np.concatenate(parts), wide


PLACES, TABLES, WIDE = onehot_tables()


def mm(left, right):
    return jnp.dot(left, right, preferred_element_type=F32)


def mm_nt(left, right):
    return lax.dot_general(left, right, (((1,), (1,)), ((), ())), preferred_element_type=F32)


def kernel(
    feats_h, wc_h, wd_h, cot_h, tab_h, wide_h, own_h, slot_h,
    pooled_o, dfeats_o, sums_o,
    feats, wc, wd, cot, tab, wide, own_s, slot_s, bf, bg, wf, wb, gh, hid, gpt, cotp, dwf,
    sx, rx, oy, sy, ry, oz, sz, rz, oyi, syi, ryi, ozi, szi, rzi, ogz, sgz, rgz, ogy, sgy, rgy, ogx, sgx, rgx,
    ogyi, sgyi, rgyi, ogxi, sgxi, rgxi,
    s1, r1, s2, r2, r3, fin,
    lsem, hs, hr, cs, cr, xs, xr, vs, vr, as_, ar, fs, fr,
):
    pos = lax.axis_index("space")
    rep = lax.axis_index("rep")
    core = lax.rem(pos, 2)
    zpos = lax.rem(lax.div(pos, 2), 8)
    xpos = lax.div(pos, 16)
    plane = xpos * 4 + rep
    sibling = pos + 1 - 2 * core

    def in_space(to):
        return {"space": to, "rep": rep}

    def in_plane(k):
        to = lax.rem(plane + k, N_PLANE)
        return {"space": lax.div(to, 4) * 16 + lax.rem(pos, 16), "rep": lax.rem(to, 4)}

    def in_z(k):
        to = lax.rem(zpos + k, N_Z)
        return {"space": xpos * 16 + to * 2 + core, "rep": rep}

    loads = [
        pltpu.make_async_copy(src, dst, lsem.at[i])
        for i, (src, dst) in enumerate(
            (
                (own_h, own_s), (slot_h, slot_s), (feats_h, feats), (tab_h, tab),
                (cot_h, cot), (wc_h, wc), (wd_h, wd), (wide_h, wide),
            )
        )
    ]
    for one in loads[:3]:
        one.start()

    barrier = pltpu.get_barrier_semaphore()
    for t in SHIFTS:
        to = lax.rem(pos + t + N_SPACE, N_SPACE)
        pl.semaphore_signal(barrier, inc=1, device_id=in_space(to), device_id_type=MESH)
    pl.semaphore_signal(barrier, inc=1, device_id=in_space(sibling), device_id_type=MESH)

    def greet_plane(k, carry):
        pl.semaphore_signal(barrier, inc=1, device_id=in_plane(k), device_id_type=MESH)
        return carry

    def greet_z(k, carry):
        pl.semaphore_signal(barrier, inc=1, device_id=in_z(k), device_id_type=MESH)
        return carry

    lax.fori_loop(1, N_PLANE, greet_plane, 0)
    lax.fori_loop(1, N_Z, greet_z, 0)

    loads[0].wait()
    loads[1].wait()

    owners = [[own_s[0, b, d] for d in range(6)] for b in range(4)]
    slots = [[slot_s[0, b, d] for d in range(6)] for b in range(4)]

    def pick(d, t):
        found = jnp.int32(0)
        for b in range(1, 4):
            hit = (owners[b][d] == pos + t) & (owners[b][d] >= 0)
            found = jnp.where(hit, b, found)
        return found

    def place(d, b):
        gap = pos - owners[b][d]
        far = jnp.clip(jnp.where(gap < 0, gap + 2, gap + 1), 0, 3)
        near = jnp.clip(5 + slots[b][d], 5, 8)
        return jnp.where(owners[b][d] < 0, 4, jnp.where(gap == 0, near, far))

    for ref in (rx, ry, rz, ryi, rzi, rgz, rgy, rgx, rgyi, rgxi):
        ref[4] = jnp.zeros(ref.shape[1:], BF)

    def halo_copy(phase, i, send, recv):
        to = lax.rem(pos + SHIFTS[i] + N_SPACE, N_SPACE)
        return pltpu.make_async_remote_copy(
            src_ref=send.at[i],
            dst_ref=recv.at[i],
            send_sem=hs.at[phase, i],
            recv_sem=hr.at[phase, i],
            device_id=in_space(to),
            device_id_type=MESH,
        )

    sent = []

    def halo_send(phase, axis, own, send, recv):
        copies = []
        for i, t in enumerate(SHIFTS):
            for side in range(2):
                send[i, side] = own(side, pick(2 * axis + side, t))
            one = halo_copy(phase, i, send, recv)
            one.start()
            copies.append(one)
        sent.extend(copies)
        return copies

    def halo_recv(axis, copies, recv):
        for one in copies:
            one.wait_recv()
        return [
            [recv[place(2 * axis + 1 - side, b), side] for b in range(4)] for side in range(2)
        ]

    def onehot(name):
        start, rows, cols = PLACES[name]
        return tab[start : start + rows, 0:cols]

    def permuted(name, value):
        return mm(onehot(name), value).astype(BF)

    loads[2].wait()
    for b in range(4):
        rx[5 + b, 0] = feats[b, 448:512, :]
        rx[5 + b, 1] = feats[b, 0:64, :]
    for side in range(2):
        for i, t in enumerate(SHIFTS):
            rows = slice(448, 512) if side == 0 else slice(0, 64)
            sx[i, side] = feats[pick(side, t), rows, :]
    pl.semaphore_wait(barrier, 4 + 1 + N_PLANE - 1 + N_Z - 1)
    copies = [halo_copy(0, i, sx, rx) for i in range(4)]
    for one in copies:
        one.start()
    sent.extend(copies)

    for one in loads[3:]:
        one.start()
    loads[3].wait()

    def x_layer(s, chunk, halo):
        rows = []
        for xq in range(4):
            x = 2 * xq + s - 1
            for b in range(4):
                if x < 0 or x > 7:
                    rows.append(halo[0 if x < 0 else 1][b][16 * chunk : 16 * chunk + 16])
                else:
                    rows.append(feats[b, 64 * x + 16 * chunk : 64 * x + 16 * chunk + 16, :])
        return jnp.concatenate(rows, axis=0)

    def put_rows(ref, y, z, count, lanes, value):
        ref[pl.ds(y * 10 + z, count), :, lanes] = value

    for chunk in range(4):
        both = jnp.concatenate([x_layer(1, chunk, None), x_layer(2, chunk, None)], axis=1)
        out = permuted("swap", both).reshape(2, 8, 16, 256)
        for j in range(2):
            put_rows(bf, 2 * chunk + j + 1, 1, 8, slice(128, 384), out[j])

    def inner_faces(ref, at, own, recv):
        for side in range(2):
            flat = jnp.concatenate([ref[i, :, 128:384] for i in at(side)], axis=0)
            faces = permuted("move", flat).reshape(4, 32, 256)
            own[side] = faces
            recv[5:9, side] = faces

    inner_faces(bf, lambda side: [(8 - 7 * side) * 10 + z for z in range(1, 9)], oyi, ryi)
    copies_y = halo_send(6, 1, lambda side, b: oyi[side, b], syi, ryi)
    inner_faces(bf, lambda side: [y * 10 + 8 - 7 * side for y in range(1, 9)], ozi, rzi)
    copies_z = halo_send(7, 2, lambda side, b: ozi[side, b], szi, rzi)

    halo = halo_recv(0, copies, rx)
    def rim_faces(out, count, own, recv):
        faces = out.astype(BF).reshape(2, 4, count, 128)
        for side in range(2):
            own[side] = faces[side]
            recv[5:9, side] = faces[side]

    ends = [[halo[end][b][rows] for end in range(2) for b in range(4)]
            for rows in (slice(48, 64), slice(0, 16))]
    rim_faces(mm(onehot("send_y"), jnp.concatenate(ends[0] + ends[1], axis=0)), 16, oy, ry)
    copies = halo_send(1, 1, lambda side, b: oy[side, b], sy, ry)
    x_halo = [halo[end][b] for end in range(2) for b in range(4)]

    for chunk in range(4):
        both = jnp.concatenate([x_layer(0, chunk, halo), x_layer(3, chunk, halo)], axis=1)
        out = permuted("swap", both).reshape(2, 8, 16, 256)
        for j in range(2):
            put_rows(bf, 2 * chunk + j + 1, 1, 8, slice(0, 128), out[j, :, :, 0:128])
            put_rows(bf, 2 * chunk + j + 1, 1, 8, slice(384, 512), out[j, :, :, 128:256])

    for one in loads[4:]:
        one.wait()
    cot_rows = jnp.concatenate(
        [cot[b, 16 * xq : 16 * xq + 16, :] for xq in range(4) for b in range(4)], axis=0
    )
    cot_perm = permuted("swap", cot_rows)
    cotp[...] = cot_perm

    def down_weight(j, k):
        return jnp.concatenate([wd[2 * j + k], wd[4 + 2 * j + k]], axis=0)

    for j in range(2):
        for k in range(2):
            out = mm_nt(cot_perm, down_weight(j, k)).reshape(4, 4, 16, 256)
            for zq in range(4):
                gh[j, 2 * zq + k] = out[:, zq]

    def weights(k9, carry):
        for s in range(4):
            for xl in range(2):
                dx = s - xl
                fwd_at = (pl.ds(s * 128, 128), pl.ds(xl * 128, 128))
                bwd_at = (pl.ds(xl * 128, 128), pl.ds(s * 128, 128))
                if 0 <= dx <= 2:
                    wf[(k9,) + fwd_at] = wc[9 * dx + k9]
                    wb[(k9,) + bwd_at] = wc[9 * (2 - dx) + 8 - k9]
                else:
                    wf[(k9,) + fwd_at] = jnp.zeros((128, 128), BF)
                    wb[(k9,) + bwd_at] = jnp.zeros((128, 128), BF)
        return carry

    lax.fori_loop(0, 9, weights, 0)

    def both_sides(make):
        return jnp.concatenate([make(0), make(1)], axis=1)

    def inner_halo(axis, copies, recv):
        halo = halo_recv(axis, copies, recv)
        return [permuted("back", jnp.concatenate(halo[side], axis=0)) for side in range(2)]

    def rim_rows(inside, halo, rows):
        def one(side):
            pad = jnp.zeros((rows - 256 - 4 * halo[side][0].shape[0], 128), BF)
            parts = [inside[side][:, 0:128], inside[side][:, 128:256], *halo[side], pad]
            return jnp.concatenate(parts, axis=0)

        return both_sides(one)

    inside = inner_halo(1, copies_y, ryi)
    for side in range(2):
        put_rows(bf, 9 * side, 1, 8, slice(128, 384), inside[side].reshape(8, 16, 256))
    corner_tiles = [
        inside[edge][16 * z : 16 * z + 16, 128 * s : 128 * s + 128]
        for z in (7, 0) for edge in range(2) for s in range(2)
    ]
    early = mm(wide[0:384, 0:640], jnp.concatenate(x_halo + corner_tiles, axis=0))
    halo = halo_recv(1, copies, ry)

    late = jnp.concatenate([halo[side][b] for side in range(2) for b in range(4)], axis=0)
    rim_faces(early + mm(wide[0:384, 640:768], late), 48, oz, rz)
    copies = halo_send(2, 2, lambda side, b: oz[side, b], sz, rz)
    out = permuted("recv_y", rim_rows(inside, halo, 384)).reshape(2, 8, 16, 256)
    for side in range(2):
        lanes = slice(128 * side, 128 * side + 128)
        put_rows(bf, 9 * side, 1, 8, slice(0, 128), out[0, :, :, lanes])
        put_rows(bf, 9 * side, 1, 8, slice(384, 512), out[1, :, :, lanes])

    inside = inner_halo(2, copies_z, rzi)
    for side in range(2):
        for y in range(1, 9):
            bf[y * 10 + 9 * side, :, 128:384] = inside[side][16 * y - 16 : 16 * y]
    bg[100:112] = jnp.zeros((12, 16, 512), BF)
    dwf[2, 1, 5] = jnp.zeros((128, 128), F32)
    def window(ref, y, z, count):
        lower = ref[pl.ds(y * 10 + z, count)]
        upper = ref[pl.ds(y * 10 + 10 + z, count)]
        return jnp.concatenate([lower, upper], axis=0).reshape(32 * count, 512)

    def activate(pre, grad):
        sig = 1.0 / (1.0 + jnp.exp(-pre))
        hidden = (pre * sig).astype(BF).reshape(-1, 16, 256)
        grad = (grad * sig * (1.0 + pre * (1.0 - sig))).astype(BF)
        return hidden, grad.reshape(-1, 16, 256)

    def inner(yq, carry):
        pre = jnp.zeros((192, 256), F32)
        for k9 in range(9):
            pre = pre + mm(window(bf, 2 * yq + k9 // 3, 1 + k9 % 3, 6), wf[k9])
        grad = jnp.concatenate([gh[j, 1:7, yq] for j in range(2)], axis=0).reshape(192, 256)
        hidden, grad = activate(pre, grad)
        for j in range(2):
            hid[j, 1:7, yq] = hidden[6 * j : 6 * j + 6]
            bg[pl.ds((2 * yq + j + 1) * 10 + 2, 6), :, 128:384] = grad[6 * j : 6 * j + 6]
        return carry

    lax.fori_loop(0, 4, inner, 0)

    middle = [(y, z) for y in range(8) for z in range(1, 7)]
    outer = [(y, z) for y in range(8) for z in (0, 7)]
    groups = [middle[0:16], middle[16:32], middle[32:48], outer]

    def tiles(ref, group, dy, dz):
        return jnp.concatenate([ref[(y + dy) * 10 + z + dz] for y, z in group], axis=0)

    def turn(at):
        gpt[at] = tiles(bg, groups[at], 1, 1)[:, 128:384].astype(F32).T.astype(BF)

    def grad_conv(part, chosen, last):
        for dz in range(3):
            first = jnp.zeros((256, 256), F32)
            second = jnp.zeros((256, 256), F32)
            for at in chosen:
                rows = tiles(bf, groups[at], part, dz)
                first = first + mm(gpt[at], rows[:, 0:256])
                second = second + mm(gpt[at], rows[:, 256:512])
            taps = (
                first[0:128, 0:128] + first[128:256, 128:256],
                first[0:128, 128:256] + second[128:256, 0:128],
                second[0:128, 0:128] + second[128:256, 128:256],
            )
            for dx in range(3):
                slot = dx * 3 + dz
                to = (part, slot // 6, slot % 6)
                dwf[to] = (dwf[to] + taps[dx]).T if last else taps[dx]

    for at in range(3):
        turn(at)
    for part in range(3):
        grad_conv(part, (0, 1, 2), False)

    halo = halo_recv(2, copies, rz)
    out = permuted("recv_z", rim_rows(inside, halo, 512)).reshape(24, 16, 256)
    for side in range(2):
        lanes = slice(128 * side, 128 * side + 128)
        for y in range(10):
            bf[y * 10 + 9 * side, :, 0:128] = out[y, :, lanes]
            bf[y * 10 + 9 * side, :, 384:512] = out[10 + y, :, lanes]
        for i, y in enumerate((0, 9)):
            bf[y * 10 + 9 * side, :, 128:256] = out[20 + i, :, lanes]
            bf[y * 10 + 9 * side, :, 256:384] = out[22 + i, :, lanes]

    pre = jnp.zeros((256, 256), F32)
    for k9 in range(9):
        pre = pre + mm(tiles(bf, outer, k9 // 3, k9 % 3), wf[k9])
    grad = jnp.concatenate([gh[y % 2, z, y // 2] for y, z in outer], axis=0)
    hidden, grad = activate(pre, grad)
    for at, (y, z) in enumerate(outer):
        hid[y % 2, z, y // 2] = hidden[at]
        bg[(y + 1) * 10 + z + 1, :, 128:384] = grad[at]

    for side in range(2):
        z = 8 if side == 0 else 1
        flat = jnp.concatenate([bg[y * 10 + z, :, 128:384] for y in range(1, 9)], axis=0)
        faces = permuted("move", flat).reshape(4, 32, 256)
        ogz[side] = faces
        rgz[5:9, side] = faces
    copies = halo_send(3, 2, lambda side, b: ogz[side, b], sgz, rgz)

    def core_copy(part):
        return pltpu.make_async_remote_copy(
            src_ref=s1.at[part], dst_ref=r1.at[part], send_sem=cs.at[part], recv_sem=cr.at[part],
            device_id=in_space(sibling), device_id_type=MESH,
        )

    def core_send(part):
        s1[part] = dwf[part, 1 - core].reshape(768, 128).astype(BF)
        core_copy(part).start()

    def each(count, act):
        def body(k, carry):
            act(k)
            return carry

        lax.fori_loop(1, count, body, 0)

    plane_group, z_group = (N_PLANE, plane, in_plane), (N_Z, zpos, in_z)
    order = [(plane_group, z_group)] * 3

    def chunk(part, index):
        size = 48 // order[part][0][0]
        return pl.ds(index * size, size)

    def scatter_copy(part, k):
        count, mine, to = order[part][0]
        return pltpu.make_async_remote_copy(
            src_ref=s2.at[part, chunk(part, lax.rem(mine + k, count))],
            dst_ref=r2.at[part, chunk(part, mine)],
            send_sem=xs.at[part], recv_sem=xr.at[part],
            device_id=to(k), device_id_type=MESH,
        )

    def sum_copy(part, k):
        _, mine, to = order[part][1]
        block = r3.at[part, chunk(part, mine)]
        return pltpu.make_async_remote_copy(
            src_ref=block, dst_ref=block, send_sem=vs.at[part], recv_sem=vr.at[part],
            device_id=to(k), device_id_type=MESH,
        )

    def gather_copy(part, k):
        _, mine, to = order[part][0]
        return pltpu.make_async_remote_copy(
            src_ref=fin.at[part, chunk(part, 0)], dst_ref=sums_o.at[part, core, chunk(part, mine)],
            send_sem=as_.at[part], recv_sem=ar.at[part],
            device_id=to(k), device_id_type=MESH,
        )

    def hand_copy(part):
        half = sums_o.at[part, core]
        return pltpu.make_async_remote_copy(
            src_ref=half, dst_ref=half, send_sem=fs.at[part], recv_sem=fr.at[part],
            device_id=in_space(sibling), device_id_type=MESH,
        )

    def all_bytes(ref, sem):
        pltpu.make_async_copy(ref, ref, sem).wait()

    def sent_bytes(part, stage):
        size = 48 // order[part][0][0]
        return pl.ds(0, size * (order[part][stage][0] - 1))

    def added(ref, part, count):
        total = ref[part, chunk(part, 0)].astype(F32)
        for i in range(1, count):
            total = total + ref[part, chunk(part, i)].astype(F32)
        return total.astype(BF)

    def scatter_send(part):
        core_copy(part).wait_recv()
        mine = dwf[part, core].reshape(768, 128) + r1[part].astype(F32)
        s2[part] = mine.astype(BF).reshape(48, 16, 128)
        count, index, _ = order[part][0]
        each(count, lambda k: scatter_copy(part, k).start())
        r2[part, chunk(part, index)] = s2[part, chunk(part, index)]

    def sum_send(part):
        all_bytes(r2.at[part, sent_bytes(part, 0)], xr.at[part])
        count, index, _ = order[part][1]
        r3[part, chunk(part, index)] = added(r2, part, order[part][0][0])
        each(count, lambda k: sum_copy(part, k).start())

    def gather_send(part):
        all_bytes(r3.at[part, sent_bytes(part, 1)], vr.at[part])
        count, index, _ = order[part][0]
        total = added(r3, part, order[part][1][0])
        fin[part, chunk(part, 0)] = total
        each(count, lambda k: gather_copy(part, k).start())
        sums_o[part, core, chunk(part, index)] = total

    def hand_over(part):
        all_bytes(sums_o.at[part, core, sent_bytes(part, 0)], ar.at[part])
        hand_copy(part).start()

    def finish(part):
        hand_copy(part).wait_recv()
        core_copy(part).wait_send()
        all_bytes(s2.at[part, sent_bytes(part, 0)], xs.at[part])
        all_bytes(r3.at[part, sent_bytes(part, 1)], vs.at[part])
        all_bytes(sums_o.at[part, core, sent_bytes(part, 0)], as_.at[part])
        hand_copy(part).wait_send()

    def down_rows(j, k):
        tiles = [hid[j, 2 * zq + k, yq] for yq in range(4) for zq in range(4)]
        return jnp.concatenate(tiles, axis=0)

    cot_t = cotp[...].astype(F32).T.astype(BF)
    for j in range(2):
        for k in range(2):
            out = mm(cot_t, down_rows(j, k))
            for i in range(2):
                tap = 4 * i + 2 * j + k
                dwf[tap // 3, 1, 3 + tap % 3] = out[:, 128 * i : 128 * i + 128].T
    turn(3)
    for part in range(3):
        grad_conv(part, (3,), True)
        core_send(part)
        if part > 0:
            scatter_send(part - 1)

    inner_faces(bg, lambda side: [(8 - 7 * side) * 10 + z for z in range(1, 9)], ogyi, rgyi)
    copies_y = halo_send(8, 1, lambda side, b: ogyi[side, b], sgyi, rgyi)
    within = [y * 10 + z for y in range(1, 9) for z in range(1, 9)]
    rim = [*range(0, 10), *range(90, 100), *range(10, 90, 10), *range(19, 90, 10)]
    rim += list(range(100, 112))

    def inside_rows(group):
        return jnp.concatenate([bg[i, :, 128:384] for i in group], axis=0)

    for group in range(4):
        rows = slice(16 * group, 16 * group + 16)
        out = permuted("send_gx", inside_rows(within[rows]))
        for b in range(4):
            for side in range(2):
                lanes = slice(128, 256) if side == 0 else slice(0, 128)
                face = out[64 * side + 16 * b : 64 * side + 16 * b + 16, lanes]
                ogxi[side, b, rows] = face
                rgxi[5 + b, side, rows] = face
    copies_x = halo_send(9, 0, lambda side, b: ogxi[side, b], sgxi, rgxi)

    scatter_send(2)

    halo = halo_recv(2, copies, rgz)
    ends = [
        halo[zs][b][rows, 128 * xl : 128 * xl + 128]
        for rows in (slice(16, 32), slice(0, 16))
        for zs in range(2) for b in range(4) for xl in range(2)
    ]
    rim_faces(mm(onehot("send_gy"), jnp.concatenate(ends, axis=0)), 16, ogy, rgy)
    copies = halo_send(4, 1, lambda side, b: ogy[side, b], sgy, rgy)
    inside_z = [permuted("back", jnp.concatenate(halo[zs], axis=0)) for zs in range(2)]
    inside_y = inner_halo(1, copies_y, rgyi)
    for side in range(2):
        for y in range(1, 9):
            bg[y * 10 + 9 * side, :, 128:384] = inside_z[side][16 * y - 16 : 16 * y]
        put_rows(bg, 9 * side, 1, 8, slice(128, 384), inside_y[side].reshape(8, 16, 256))
    early = mm(wide[384:768, 0:512], jnp.concatenate(inside_y + inside_z, axis=0))

    def shift_rows(group):
        rows = inside_rows(group)
        lower = permuted("low", rows[:, 128:256]).reshape(16, 16, 128)
        upper = permuted("high", rows[:, 0:128]).reshape(16, 16, 128)
        for at, i in enumerate(group):
            bg[i, :, 0:128] = lower[at]
            bg[i, :, 384:512] = upper[at]

    def insert_rows(group, halo, rows):
        layers = [halo[side][b][rows] for side in range(2) for b in range(4)]
        out = permuted("insert", jnp.concatenate(layers, axis=0)).reshape(32, 16, 128)
        for at, i in enumerate(group):
            bg[i, :, 0:128] = bg[i, :, 0:128] + out[at]
            bg[i, :, 384:512] = bg[i, :, 384:512] + out[16 + at]

    for group in range(4):
        shift_rows(within[16 * group : 16 * group + 16])
    total = jnp.zeros((256, 128), F32)
    for j in range(2):
        for k in range(2):
            total = total + mm(down_rows(j, k), down_weight(j, k))
    out = permuted("swap", total.astype(BF))
    for b in range(4):
        for xq in range(4):
            at = 16 * (4 * xq + b)
            pooled_o[b, 16 * xq : 16 * xq + 16, :] = out[at : at + 16]
    sum_send(0)
    sum_send(1)
    halo = halo_recv(1, copies, rgy)
    late = jnp.concatenate([halo[side][b] for side in range(2) for b in range(4)], axis=0)
    late = mm(wide[384:768, 512:640], late)
    faces = (early[0:192, 128:256] + late[0:192], early[192:384, 0:128] + late[192:384])
    rim_faces(jnp.concatenate(faces, axis=0), 48, ogx, rgx)
    copies = halo_send(5, 0, lambda side, b: ogx[side, b], sgx, rgx)
    corners = both_sides(lambda side: jnp.concatenate(halo[side], axis=0))
    corners = jnp.concatenate([corners, jnp.zeros((64, 256), BF)], axis=0)
    out = permuted("recv_gy", corners).reshape(2, 2, 16, 256)
    for side in range(2):
        for zs in range(2):
            for xl in range(2):
                lanes = slice(128 + 128 * xl, 256 + 128 * xl)
                face = out[xl, zs, :, 128 * side : 128 * side + 128]
                bg[90 * side + 9 * zs, :, lanes] = face
    for group in range(3):
        shift_rows(rim[16 * group : 16 * group + 16])
    sum_send(2)
    halo = halo_recv(0, copies_x, rgxi)
    for group in range(4):
        rows = slice(16 * group, 16 * group + 16)
        insert_rows(within[rows], halo, rows)
    gather_send(0)
    gather_send(1)
    halo = halo_recv(0, copies, rgx)
    for group in range(3):
        rows = slice(16 * group, 16 * group + 16)
        insert_rows(rim[rows], halo, rows)

    def backward(yq, carry):
        grad = jnp.zeros((256, 256), F32)
        for k9 in range(9):
            grad = grad + mm_nt(window(bg, 2 * yq + k9 // 3, k9 % 3, 8), wb[k9])
        out = permuted("swap", grad.astype(BF))
        for xq in range(4):
            for b in range(4):
                tile = out[16 * (4 * xq + b) : 16 * (4 * xq + b) + 16]
                for xl in range(2):
                    at = pl.ds(pl.multiple_of(64 * (2 * xq + xl) + 16 * yq, 16), 16)
                    dfeats_o[b, at, :] = tile[:, 128 * xl : 128 * xl + 128]
        return carry

    gather_send(2)
    lax.fori_loop(0, 4, backward, 0)
    for part in range(3):
        hand_over(part)
    for one in sent:
        one.wait_send()
    for part in range(3):
        finish(part)


def epilogue(norm, sums, pooled, dfeats, pooled_o, dfeats_o, conv_o, down_o, conv, down, sem):
    copies = [
        pltpu.make_async_copy(dfeats, dfeats_o, sem.at[0]),
        pltpu.make_async_copy(pooled, pooled_o, sem.at[1]),
    ]
    copies[0].start()
    copies[1].start()
    for part in range(3):
        conv[part] = (sums[part, 0:9].astype(F32) * norm).reshape(3, 3, 128, 128)
        one = pltpu.make_async_copy(conv.at[part], conv_o.at[:, part], sem.at[2 + part])
        one.start()
        copies.append(one)
    for tap in range(8):
        down[tap] = sums[tap // 3, 9 + tap % 3].astype(F32) * norm
    one = pltpu.make_async_copy(down, down_o, sem.at[5])
    one.start()
    copies.append(one)
    for one in copies:
        one.wait()


def per_device(feats, w_conv, w_down, cotangent, nbr_owner, nbr_slot):
    def buf(*shape, dtype=BF):
        return pltpu.VMEM(shape, dtype)

    def halo(rows, lanes, own=True):
        bufs = [buf(4, 2, rows, lanes), buf(9, 2, rows, lanes)]
        return ([buf(2, 4, rows, lanes)] if own else []) + bufs

    def in_hbm(value):
        return pltpu.with_memory_space_constraint(value, pltpu.HBM)

    vmem = pl.BlockSpec(memory_space=pltpu.VMEM)
    hbm = pl.BlockSpec(memory_space=pltpu.HBM)
    dma = pltpu.SemaphoreType.DMA
    operands = (
        feats[0], w_conv, w_down, cotangent[0], jnp.asarray(TABLES, BF), jnp.asarray(WIDE, BF),
        nbr_owner, nbr_slot,
    )
    pooled, d_feats, sums = pl.pallas_call(
        kernel,
        out_shape=(
            pltpu.VMEM((4, 64, 128), BF),
            pltpu.VMEM((4, 512, 128), BF),
            pltpu.VMEM((3, 2, 48, 16, 128), BF),
        ),
        in_specs=[hbm] * 8,
        out_specs=(vmem, vmem, vmem),
        scratch_shapes=[
            buf(4, 512, 128), buf(27, 128, 128), buf(8, 128, 128), buf(4, 64, 128),
            buf(*TABLES.shape), buf(*WIDE.shape),
            pltpu.SMEM((1, 4, 6), jnp.int32), pltpu.SMEM((1, 4, 6), jnp.int32),
            buf(100, 16, 512), buf(112, 16, 512),
            buf(9, 512, 256), buf(9, 256, 512),
            buf(2, 8, 4, 16, 256, dtype=F32), buf(2, 8, 4, 16, 256),
            buf(4, 256, 256), buf(256, 128),
            buf(3, 2, 6, 128, 128, dtype=F32),
            *halo(64, 128, own=False), *halo(16, 128), *halo(48, 128),
            *halo(32, 256), *halo(32, 256),
            *halo(32, 256), *halo(16, 128), *halo(48, 128),
            *halo(32, 256), *halo(64, 128),
            buf(3, 768, 128), buf(3, 768, 128),
            buf(3, 48, 16, 128), buf(3, 48, 16, 128), buf(3, 96, 16, 128), buf(3, 6, 16, 128),
            dma((8,)),
            dma((10, 4)), dma((10, 4)),
            *([dma((3,))] * 10),
        ],
        compiler_params=pltpu.CompilerParams(
            collective_id=0, has_side_effects=True, vmem_limit_bytes=48 * 1024 * 1024
        ),
    )(*[in_hbm(one) for one in operands])
    norm = 1.0 / float(lax.axis_size("rep") * lax.axis_size("space") * 4 * 512) ** 0.5
    pooled, d_feats, conv, down = pl.pallas_call(
        functools.partial(epilogue, norm),
        out_shape=(
            jax.ShapeDtypeStruct((4, 64, 128), BF),
            jax.ShapeDtypeStruct((4, 512, 128), BF),
            jax.ShapeDtypeStruct((3, 3, 3, 128, 128), F32),
            jax.ShapeDtypeStruct((8, 128, 128), F32),
        ),
        in_specs=[vmem] * 3,
        out_specs=[hbm] * 4,
        scratch_shapes=[buf(3, 3, 3, 128, 128, dtype=F32), buf(8, 128, 128, dtype=F32), dma((6,))],
        compiler_params=pltpu.CompilerParams(vmem_limit_bytes=24 * 1024 * 1024),
    )(sums.reshape(3, 12, 128, 128), pooled, d_feats)
    return (pooled[None], d_feats[None], conv.reshape(27, 128, 128), down)


def solution(mesh):
    placed = (
        P("rep", "space", None, None),
        P(),
        P(),
        P("rep", "space", None, None),
        P("rep", "space", None),
        P("rep", "space", None),
    )
    return jax.shard_map(
        per_device,
        mesh=mesh,
        in_specs=placed,
        out_specs=(P("rep", "space", None, None), P("rep", "space", None, None), P(), P()),
        check_vma=False,
    )
```
